32 devices in a mesh: stream: 8 (over z, core), girth: 4 (over y, x).
Axes of the slice: x: 2, y: 2, z: 4, core: 2. Of those that a mesh axis runs over, the one named last changes fastest.
Arguments:
- state: float32 [16, 7, 32, 128], P('stream', None, 'girth'), may hold values from -1.8 to 1.8
- propeller: float32 [7, 8192], P(None, ('stream', 'girth')), may hold values from -6 to 6
- donor_index: int32 [32, 32], P(('stream', 'girth')), may hold values from -1 to 255, as said below
- fringe_index: int32 [32, 32], P(('stream', 'girth')), may hold values from -1 to 2047, as said below
- donor_weight: float32 [32, 32], P(('stream', 'girth')), may hold values from 0.25 to 1
- disk_mask: int32 [16, 32, 128], P('stream', 'girth'), may hold values 0 or 1
- thrust: float32 [7], replicated, may hold values from -1.8 to 1.8
- face: float32 [16, 6, 32, 128], P('stream', None, 'girth'), may hold values from 0.2 to 1
- coupling: float32 [6, 7, 7], replicated, may hold values from -0.875 to 0.875
- diag_inverse: bfloat16 [16, 7, 7, 32, 128], P('stream', None, None, 'girth'), may hold values from -0.15039062 to 1
- lower_jacobian: float32 [7, 7], replicated, may hold values from -0.06 to 1.06
- upper_jacobian: float32 [7, 7], replicated, may hold values from -0.06 to 1.06
Outputs:
- new_state: float32 [16, 7, 32, 128], P('stream', None, 'girth')
- residual: float32 [16, 7, 32, 128], P('stream', None, 'girth')
The draws below stay inside these ranges and needn't reach their ends.
Inputs may be any that keep to these rules, and one draw needn't show every extreme that they name: `donor_index`: live slots of one device and peer come first; every device of one streamwise index fills all 8 slots toward one common peer. `fringe_index`: equal to -1 exactly where donor_index is -1.
All inputs are finite; a program needn't handle non-finite values. No bound on the sum of `disk_mask` on one device may be relied on, other than what follows from the above.
Results may differ from the reference program's by a relative error of at most 0.0003.
Values sent between devices are 32-bit elements; how exact they have to be, the bound alone decides.
A program may use at most 64 MiB of HBM per device.

```python
import math
import jax
import jax.numpy as jnp
from jax import lax

VARS = 7
CS = 2
CG = 8
CN = 128
PROP_DEV = 256
CAP = 8
STREAM_CELLS = 16
NG = 32
SENDERS = 32
PROP = 8192
N_STREAM = 8
N_GIRTH = 4


def overset_layout(key):
    base = jax.random.fold_in(key, 17)
    entry_counts = jax.random.randint(jax.random.fold_in(base, 1), (N_STREAM, N_GIRTH, N_GIRTH), 1, CAP + 1)
    busy_peer = jax.random.randint(jax.random.fold_in(base, 2), (N_STREAM, 1, 1), 0, N_GIRTH)
    peer_index = jnp.arange(N_GIRTH)[None, None, :]
    sender_index = jnp.arange(N_GIRTH)[None, :, None]
    entry_counts = jnp.where(peer_index == busy_peer, CAP, entry_counts)
    quiet_peer = (busy_peer + 1) % N_GIRTH
    entry_counts = jnp.where((sender_index == 0) & (peer_index == quiet_peer), 1, entry_counts)
    position_index = jnp.arange(CAP)[None, None, None, :]
    is_live = position_index < entry_counts[..., None]
    marked = ((sender_index == 0) & (peer_index == busy_peer))[..., None]
    return (is_live, marked, position_index)


def draw_donor_index(key, part):
    is_live, marked, position_index = overset_layout(key)
    chosen = jax.random.randint(jax.random.fold_in(key, 21), is_live.shape, 0, PROP_DEV)
    chosen = jnp.where(marked & (position_index == 0), PROP_DEV - 1, chosen)
    chosen = jnp.where(marked & (position_index == 1), 0, chosen)
    result = jnp.where(is_live, chosen, -1)
    return result.reshape(N_STREAM * N_GIRTH, N_GIRTH * CAP).astype(jnp.int32)


def draw_fringe_index(key, part):
    is_live, marked, position_index = overset_layout(key)
    chosen = jax.random.randint(jax.random.fold_in(key, 23), is_live.shape, 0, CS * CG * CN)
    chosen = jnp.where(marked & (position_index == 0), CS * CG * CN - 1, chosen)
    chosen = jnp.where(marked & (position_index == 1), 0, chosen)
    result = jnp.where(is_live, chosen, -1)
    return result.reshape(N_STREAM * N_GIRTH, N_GIRTH * CAP).astype(jnp.int32)


def draw_diag_inverse(key, part):
    full_shape = (STREAM_CELLS, 7, 7, NG, CN)
    first_key = jax.random.fold_in(key, 31)
    second_key = jax.random.fold_in(key, 32)
    tertiary_key = jax.random.fold_in(key, 33)
    diagonal = jax.random.uniform(first_key, (STREAM_CELLS, 7, 1, NG, CN), jnp.float32, 0.9, 1.0)
    off_diagonal = jnp.clip(0.035 * jax.random.normal(second_key, full_shape, jnp.float32), -0.15, 0.15)
    packet_groups = jax.random.randint(tertiary_key, (3,), 0, STREAM_CELLS)
    packet_rows = jnp.any(jnp.arange(STREAM_CELLS)[:, None] == packet_groups[None, :], axis=1)
    scale_factor = jnp.where(packet_rows, 0.6, 1.0).astype(jnp.float32)[:, None, None, None, None]
    unit = jnp.eye(7, dtype=jnp.float32)[None, :, :, None, None]
    return (unit * diagonal * scale_factor + (1.0 - unit) * off_diagonal).astype(jnp.bfloat16)


def draw_lower_jacobian(key, part):
    first_key = jax.random.fold_in(key, 41)
    second_key = jax.random.fold_in(key, 42)
    ranking = jax.random.permutation(first_key, 7)
    slow_channel = ranking < 4
    rates = jnp.where(slow_channel, jnp.exp(-2.3 / STREAM_CELLS), jnp.exp(-1.0 / 40.0)).astype(jnp.float32)
    off_diagonal = jnp.clip(0.015 * jax.random.normal(second_key, (7, 7), jnp.float32), -0.06, 0.06)
    unit = jnp.eye(7, dtype=jnp.float32)
    return unit * (rates / 0.95)[:, None] + (1.0 - unit) * off_diagonal


def draw_upper_jacobian(key, part):
    first_key = jax.random.fold_in(key, 51)
    second_key = jax.random.fold_in(key, 52)
    ranking = jax.random.permutation(first_key, 7)
    slow_channel = ranking < 4
    rates = jnp.where(slow_channel, jnp.exp(-2.3 / STREAM_CELLS), jnp.exp(-1.0 / 32.0)).astype(jnp.float32)
    off_diagonal = jnp.clip(0.015 * jax.random.normal(second_key, (7, 7), jnp.float32), -0.06, 0.06)
    unit = jnp.eye(7, dtype=jnp.float32)
    return unit * (rates / 0.95)[:, None] + (1.0 - unit) * off_diagonal


def plant(array, rng, least, high):
    longest = array.shape.index(max(array.shape))
    spots = []
    for shift in (0, 1):
        where = [jax.random.randint(jax.random.fold_in(rng, axis), (), 0, length) for axis, length in enumerate(array.shape)]
        where[longest] = (where[longest] + shift) % array.shape[longest]
        spots.append(tuple(where))
    return array.at[spots[0]].set(least).at[spots[1]].set(high)


def level_of(rng, extent, cuts, least, high):
    level, own = 1.0, jax.random.fold_in(rng, 6)
    for dim, blocks in cuts:
        steps = jnp.exp(jax.random.uniform(jax.random.fold_in(own, dim), (blocks,), jnp.float32, least / len(cuts), high / len(cuts)))
        level = level * jnp.repeat(steps, extent[dim] // blocks).reshape([-1 if axis == dim else 1 for axis in range(len(extent))])
    return level


def gaussian(own_key, extent, width, limit, split=(), kind=jnp.bfloat16):
    array = jax.random.normal(own_key, extent, jnp.float32) * width
    if len(split) > 0:
        array = level_of(own_key, extent, split, -0.22, 0.18) * array
    return jnp.clip(array, min=-limit, max=limit).astype(kind)


def setup_inputs(seed: int = 0) -> dict:
    streams_of = jax.random.split(jax.random.key(seed), 13)
    state = gaussian(streams_of[0], (STREAM_CELLS, VARS, NG, CN), 0.3, 1.8, ((0, 8), (2, 4)), jnp.float32)
    propeller = gaussian(streams_of[1], (VARS, PROP), 1.0, 6.0, ((1, 32),), jnp.float32)
    donor_index = draw_donor_index(jax.random.fold_in(streams_of[12], 71), 0)
    fringe_index = draw_fringe_index(jax.random.fold_in(streams_of[12], 71), 0)
    donor_weight = jnp.clip(0.25 + 0.75 * jax.random.uniform(streams_of[4], (SENDERS, N_GIRTH * CAP), jnp.float32) ** level_of(streams_of[4], (SENDERS, N_GIRTH * CAP), ((0, 32),), -0.2, 0.2), 0.25, 1.0)
    disk_mask = plant((jax.random.randint(streams_of[5], (STREAM_CELLS, NG, CN), 0, 6) < 1).astype(jnp.int32), jax.random.fold_in(streams_of[5], 1), 0, 1)
    thrust = gaussian(streams_of[6], (VARS,), 0.3, 1.8, (), jnp.float32)
    face = jnp.clip(jnp.exp(math.log(1.0) - 1.609438 * jax.random.uniform(streams_of[7], (STREAM_CELLS, 6, NG, CN), jnp.float32) ** level_of(streams_of[7], (STREAM_CELLS, 6, NG, CN), ((0, 8), (2, 4)), -0.2, 0.2)), 0.2, 1.0)
    coupling = gaussian(streams_of[8], (6, VARS, VARS), 49 ** -0.5, 0.875, (), jnp.float32)
    diag_inverse = draw_diag_inverse(jax.random.fold_in(streams_of[12], 71), 0)
    lower_jacobian = draw_lower_jacobian(jax.random.fold_in(streams_of[12], 71), 0)
    upper_jacobian = draw_upper_jacobian(jax.random.fold_in(streams_of[12], 71), 0)
    return dict(state=state, propeller=propeller, donor_index=donor_index, fringe_index=fringe_index, donor_weight=donor_weight, disk_mask=disk_mask, thrust=thrust, face=face, coupling=coupling, diag_inverse=diag_inverse, lower_jacobian=lower_jacobian, upper_jacobian=upper_jacobian)


PRECISE = lax.Precision.HIGHEST


def residual_from(current, stream_pad, beside_all, face, coupling, disk_mask, thrust):
    normal_pad = jnp.pad(current, ((0, 0), (0, 0), (0, 0), (1, 1)))
    beside = [stream_pad[:-2], stream_pad[2:], beside_all[:, :, :-2], beside_all[:, :, 2:], normal_pad[..., :-2], normal_pad[..., 2:]]
    residual = disk_mask.astype(jnp.float32)[:, None] * thrust[None, :, None, None]
    for direction in range(6):
        residual = residual + face[:, direction:direction + 1] * jnp.einsum("ij,ajbc->aibc", coupling[direction], beside[direction] - current, precision=PRECISE)
    return residual


def forward_step(matrix):
    def advance(previous, inputs):
        inverse, source = inputs
        inverse = inverse.astype(jnp.float32)
        result = jnp.einsum("ijc,jc->ic", inverse, source + jnp.dot(matrix, previous, precision=PRECISE), precision=PRECISE)
        return result, result
    return advance


def backward_step(matrix):
    def advance(following, inputs):
        inverse, star = inputs
        inverse = inverse.astype(jnp.float32)
        result = star + jnp.einsum("ijc,jc->ic", inverse, jnp.dot(matrix, following, precision=PRECISE), precision=PRECISE)
        return result, result
    return advance


def reference(state, propeller, donor_index, fringe_index, donor_weight, disk_mask, thrust, face, coupling, diag_inverse, lower_jacobian, upper_jacobian):
    all_cells = STREAM_CELLS * NG * CN
    sender_ids = jnp.arange(N_STREAM * N_GIRTH, dtype=jnp.int32)[:, None]
    is_live = donor_index >= 0
    source_cols = (sender_ids * PROP_DEV + jnp.maximum(donor_index, 0)).astype(jnp.int32).reshape(-1)
    outgoing = jnp.take(propeller, source_cols, axis=1) * jnp.where(is_live, donor_weight, 0.0).reshape(-1)[None, :]
    slab_index = sender_ids // N_GIRTH
    peer_index = jnp.arange(N_GIRTH * CAP, dtype=jnp.int32)[None, :] // CAP
    target = jnp.maximum(fringe_index, 0)
    row_index = slab_index * CS + target // (CG * CN)
    girth_index = peer_index * CG + (target % (CG * CN)) // CN
    normal_index = target % CN
    flat_index = (row_index * NG + girth_index) * CN + normal_index
    flat_index = jnp.where(is_live, flat_index, all_cells).astype(jnp.int32).reshape(-1)
    accumulated = jnp.zeros((all_cells, 7), jnp.float32).at[flat_index].add(outgoing.T, mode="drop")
    hit_count = jnp.zeros((all_cells,), jnp.int32).at[flat_index].add(1, mode="drop")
    fringe = (hit_count > 0).reshape(STREAM_CELLS, 1, NG, CN)
    donated = accumulated.reshape(STREAM_CELLS, NG, CN, 7).transpose(0, 3, 1, 2)
    current = jnp.where(fringe, donated, state)
    stream_pad = jnp.pad(current, ((1, 1), (0, 0), (0, 0), (0, 0)))
    beside_all = jnp.concatenate([current[:, :, -1:], current, current[:, :, :1]], axis=2)
    residual = residual_from(current, stream_pad, beside_all, face, coupling, disk_mask, thrust)
    source = jnp.where(fringe, 0.0, -residual).reshape(STREAM_CELLS, 7, NG * CN)
    inverse = diag_inverse.reshape(STREAM_CELLS, 7, 7, NG * CN)
    start = jnp.zeros((7, NG * CN), jnp.float32)
    _, stars = lax.scan(forward_step(lower_jacobian), start, (inverse, source))
    _, updates = lax.scan(backward_step(upper_jacobian), start, (inverse, stars), reverse=True)
    new_state = current + updates.reshape(STREAM_CELLS, 7, NG, CN)
    return new_state, residual
```

```python
import functools

import jax
import jax.numpy as jnp
from jax import lax
from jax.experimental import pallas as pl
from jax.experimental.pallas import tpu as pltpu
from jax.sharding import PartitionSpec as P

MESH = pl.DeviceIdType.MESH
PRECISE = lax.Precision.HIGHEST
VARS = 7
ROWS = 2
TEAM = 4
PAIR = 2
CAP = 8


def kernel(
    n_stream,
    n_girth,
    state,
    prop,
    donor,
    landing,
    weight,
    disk,
    thrust,
    face,
    coupling,
    inverse,
    lower,
    upper,
    new_state,
    residual_out,
    packet,
    packets,
    edge_out,
    edge_in,
    row_in,
    planes,
    inv_out,
    inv_in,
    current,
    rhs_planes,
    rhs_out,
    rhs_in,
    fmap,
    bmap,
    upd_out,
    upd_in,
    link_out,
    link_in,
    packet_sems,
    edge_sems,
    row_sems,
    inv_sems,
    rhs_sems,
    upd_sems,
    link_sems,
    local_sems,
):
    s, g = lax.axis_index("stream"), lax.axis_index("girth")
    base = (s // TEAM) * TEAM
    place = s - base
    team = s // TEAM
    n_teams = n_stream // TEAM
    slots = donor.shape[1]
    packs = n_girth if n_girth * slots <= 128 else 1

    def girth_at(k):
        return lax.rem(g + k + n_girth, n_girth)

    def remote(src, dst, sems, at, to):
        return pltpu.make_async_remote_copy(
            src_ref=src,
            dst_ref=dst,
            send_sem=sems.at[(0, *at)],
            recv_sem=sems.at[(1, *at)],
            device_id=to,
            device_id_type=MESH,
        )

    def has(ds):
        return jnp.logical_and(s + ds >= 0, s + ds < n_stream)

    barrier = pltpu.get_barrier_semaphore()

    def greet(to):
        pl.semaphore_signal(barrier, inc=1, device_id=to, device_id_type=MESH)

    for k in range(1, n_girth):
        greet((s, girth_at(k)))
    expected = n_girth - 1
    for ds in (-1, 1):

        @pl.when(has(ds))
        def _():
            for k in range(n_girth):
                greet((s + ds, girth_at(k)))

        expected = expected + jnp.where(has(ds), n_girth, 0)
    for k in range(1, TEAM):
        q = lax.rem(place + k, TEAM)
        far = jnp.logical_or(q - place > 1, place - q > 1)

        @pl.when(far)
        def _():
            greet((base + q, g))

        expected = expected + jnp.where(far, 1, 0)
    for ds in (-TEAM, TEAM):

        @pl.when(has(ds))
        def _():
            greet((s + ds, g))

        expected = expected + jnp.where(has(ds), 1, 0)

    lane = lax.broadcasted_iota(jnp.int32, (1, 128), 1)

    def spread(ref):
        return jnp.concatenate([ref[...]] * packs, axis=1) if packs > 1 else ref[...]

    donor_all = spread(donor)
    live = jnp.logical_and(lane // slots == lax.rem(g, packs), donor_all >= 0)
    cell = lax.broadcasted_iota(jnp.int32, (prop.shape[1], 128), 0)
    chosen = jnp.where(cell == jnp.where(live, donor_all, -1), 1.0, 0.0)
    taken = jnp.dot(prop[...], chosen, precision=PRECISE, preferred_element_type=jnp.float32)
    packet[0:VARS, :] = taken * jnp.where(live, spread(weight), 0.0)
    packet[VARS : VARS + 1, :] = jnp.where(live, spread(landing) + 1, 0).astype(jnp.float32)
    packets[1, 0] = packet[...]

    for side, at in ((0, 0), (1, 7)):
        for r in range(ROWS):
            edge_out[side, r, 0:VARS, :] = state[pl.ds(r * VARS * 8 + at, VARS, stride=8), :]
            edge_out[side, r, VARS : VARS + 1, :] = jnp.zeros((1, 128), jnp.float32)

    pl.semaphore_wait(barrier, expected)

    def packet_copy(ds, k):
        return remote(
            packet, packets.at[1 - ds, k], packet_sems, (1 - ds, k), (s + ds, girth_at(k))
        )

    def edge_copy(side):
        return remote(
            edge_out.at[side], edge_in.at[side], edge_sems, (side,), (s, girth_at(2 * side - 1))
        )

    def row_copy(side):
        rows = VARS * 8
        return remote(
            state.at[pl.ds(side * rows, rows)],
            row_in.at[side],
            row_sems,
            (side,),
            (s + 2 * side - 1, g),
        )

    for ds in (-1, 1):

        @pl.when(has(ds))
        def _():
            row_copy((ds + 1) // 2).start()
            for k in range(n_girth):
                packet_copy(ds, k).start()

    for side in (0, 1):
        edge_copy(side).start()
    for k in range(1, n_girth):
        packet_copy(0, k).start()

    for r in range(ROWS):
        for i in range(VARS):
            for j in range(VARS):
                p = (r * VARS + i) * VARS + j
                planes[p * 8 : p * 8 + 8, :] = inverse[r, i, j].astype(jnp.float32)
    blocks = planes.shape[0] // 64
    planes[ROWS * VARS * VARS * 8 :, :] = jnp.zeros(
        (planes.shape[0] - ROWS * VARS * VARS * 8, 128), jnp.float32
    )
    for c in range(8):
        for b in range(blocks):
            inv_out[c // PAIR, c % PAIR, b * 8 : b * 8 + 8, :] = planes[
                pl.ds(b * 64 + c, 8, stride=8), :
            ]

    def team_copy(out, into, sems, k):
        q = lax.rem(place + k, TEAM)
        return remote(out.at[q], into.at[place], sems, (k,), (base + q, g))

    def own_copy(out, into, n):
        return pltpu.make_async_copy(out.at[place], into.at[place], local_sems.at[n])

    for k in range(1, TEAM):
        team_copy(inv_out, inv_in, inv_sems, k).start()
    own_copy(inv_out, inv_in, 0).start()

    for side in (0, 1):
        edge_copy(side).wait_recv()
    for k in range(1, n_girth):
        packet_copy(0, k).wait_recv()
    for ds in (-1, 1):

        @pl.when(has(ds))
        def _():
            row_copy((1 - ds) // 2).wait_recv()
            for k in range(n_girth):
                packet_copy(-ds, k).wait_recv()

    girth_cell = lax.broadcasted_iota(jnp.int32, (8, 128), 0)
    normal_cell = lax.broadcasted_iota(jnp.int32, (8, 128), 1)
    normal_rows = lax.broadcasted_iota(jnp.int32, (128, 128), 0)
    var_row = lax.broadcasted_iota(jnp.int32, (8, 128), 0)
    peer = lax.rem(lane, slots) // CAP

    def landed(o, plan):
        total = None
        for first in range(0, n_girth, packs):
            tile = packets[o, first]
            for k in range(first + 1, first + packs):
                tile = tile + packets[o, k]
            code = tile[VARS : VARS + 1, :].astype(jnp.int32) - 1
            row, gc, nc = code >> 10, (code >> 7) & 7, code & 127
            nc = jnp.where(code >= 0, nc, -1)
            tile = jnp.where(var_row == VARS, 1.0, tile)
            part = lax.dot_general(
                jnp.concatenate(plan(tile, row, gc), axis=0),
                jnp.where(normal_rows == nc, 1.0, 0.0),
                (((1,), (1,)), ((), ())),
                precision=PRECISE,
                preferred_element_type=jnp.float32,
            )
            total = part if total is None else total + part
        return total

    def block_rows(r):
        def plan(tile, row, gc):
            here = jnp.logical_and(row == r, peer == g)
            hit = jnp.where(girth_cell == jnp.where(here, gc, -1), 1.0, 0.0)
            return [tile[v : v + 1, :] * hit for v in range(8)]

        return plan

    def own_plan(tile, row, gc):
        rows = block_rows(0)(tile, row, gc) + block_rows(1)(tile, row, gc)
        for at, side in ((7, -1), (0, 1)):
            for r in range(ROWS):
                here = (peer == girth_at(side)) & (row == r) & (gc == at)
                rows.append(tile * jnp.where(here, 1.0, 0.0))
        return rows

    def settle(found, raw):
        hit = found[VARS * 8 : VARS * 8 + 8] > 0.5
        return [jnp.where(hit, found[v * 8 : v * 8 + 8], raw(v)) for v in range(VARS)], hit

    own = landed(1, own_plan)
    cells, fringe = [], []
    for r in range(ROWS):
        found, hit = settle(
            own[r * 64 : r * 64 + 64], lambda v: state[(r * VARS + v) * 8 : (r * VARS + v) * 8 + 8, :]
        )
        cells.append(found)
        fringe.append(hit)
        for v in range(VARS):
            current[(r * VARS + v) * 8 : (r * VARS + v) * 8 + 8, :] = found[v]
    beside = {}
    for side in (0, 1):
        for r in range(ROWS):
            at = 128 + (side * ROWS + r) * 8
            found = own[at : at + 8]
            beside[side, r] = jnp.where(
                found[VARS : VARS + 1] > 0.5, found, edge_in[1 - side, r]
            )
    outer = []
    for o, r, side in ((0, 1, 1), (2, 0, 0)):
        found, _ = settle(
            landed(o, block_rows(r)), lambda v: row_in[side, v * 8 : v * 8 + 8, :]
        )
        outer.append([jnp.where(has(o - 1), x, 0.0) for x in found])

    for r in range(ROWS):
        here = cells[r]
        before = outer[0] if r == 0 else cells[r - 1]
        after = outer[1] if r == ROWS - 1 else cells[r + 1]
        in_disk = disk[r * 8 : r * 8 + 8, :].astype(jnp.float32)
        total = [in_disk * thrust[v] for v in range(VARS)]
        for d in range(6):
            step = []
            for v in range(VARS):
                x = here[v]
                if d == 0:
                    near = before[v]
                elif d == 1:
                    near = after[v]
                elif d == 2:
                    near = jnp.where(girth_cell == 0, beside[0, r][v : v + 1], pltpu.roll(x, 1, 0))
                elif d == 3:
                    near = jnp.where(girth_cell == 7, beside[1, r][v : v + 1], pltpu.roll(x, 7, 0))
                elif d == 4:
                    near = jnp.where(normal_cell == 0, 0.0, pltpu.roll(x, 1, 1))
                else:
                    near = jnp.where(normal_cell == 127, 0.0, pltpu.roll(x, 127, 1))
                step.append(near - x)
            area = face[(r * 6 + d) * 8 : (r * 6 + d) * 8 + 8, :]
            for i in range(VARS):
                flux = step[0] * coupling[d, i, 0]
                for j in range(1, VARS):
                    flux = flux + step[j] * coupling[d, i, j]
                total[i] = total[i] + area * flux
        for v in range(VARS):
            residual_out[(r * VARS + v) * 8 : (r * VARS + v) * 8 + 8, :] = total[v]
            rhs_planes[r, v * 8 : v * 8 + 8, :] = jnp.where(fringe[r], 0.0, -total[v])
        for c in range(8):
            rhs_out[c // PAIR, r, c % PAIR, 0:VARS, :] = rhs_planes[r, pl.ds(c, VARS, stride=8), :]

    for k in range(1, TEAM):
        team_copy(rhs_out, rhs_in, rhs_sems, k).start()
    own_copy(rhs_out, rhs_in, 1).start()

    for k in range(1, TEAM):
        team_copy(inv_out, inv_in, inv_sems, TEAM - k).wait_send()
        pltpu.make_async_remote_copy(
            src_ref=inv_out.at[place],
            dst_ref=inv_in.at[lax.rem(place + TEAM - k, TEAM)],
            send_sem=inv_sems.at[0, k],
            recv_sem=inv_sems.at[1, k],
            device_id=(base + lax.rem(place + k, TEAM), g),
            device_id_type=MESH,
        ).wait_recv()
    own_copy(inv_out, inv_in, 0).wait()

    def column(k, h, r, j):
        return inv_in[k, h, pl.ds(r * VARS * VARS + j, VARS, stride=VARS), :]

    def matrices(k, carry):
        for r in range(ROWS):
            for h in range(PAIR):
                cols = [column(k, h, r, j) for j in range(VARS)]
                for m in range(VARS):
                    f, b = cols[0] * lower[0, m], cols[0] * upper[0, m]
                    for j in range(1, VARS):
                        f = f + cols[j] * lower[j, m]
                        b = b + cols[j] * upper[j, m]
                    fmap[k, r, h, m, 0:VARS, :] = f
                    bmap[k, r, h, m, 0:VARS, :] = b
        return carry

    lax.fori_loop(0, TEAM, matrices, 0)

    for k in range(1, TEAM):
        team_copy(rhs_out, rhs_in, rhs_sems, TEAM - k).wait_send()
        pltpu.make_async_remote_copy(
            src_ref=rhs_out.at[place],
            dst_ref=rhs_in.at[lax.rem(place + TEAM - k, TEAM)],
            send_sem=rhs_sems.at[0, k],
            recv_sem=rhs_sems.at[1, k],
            device_id=(base + lax.rem(place + k, TEAM), g),
            device_id_type=MESH,
        ).wait_recv()
    own_copy(rhs_out, rhs_in, 1).wait()

    def product(matrix, x):
        parts = [matrix(j) * x[j : j + 1, :] for j in range(VARS)]
        return ((parts[0] + parts[1]) + (parts[2] + parts[3])) + (
            (parts[4] + parts[5]) + parts[6]
        )

    offsets = {}
    for k in range(TEAM):
        for r in range(ROWS):
            for h in range(PAIR):
                offsets[k, r, h] = product(
                    lambda j: column(k, h, r, j), rhs_in[k, r, h, 0:VARS, :]
                )

    def link_copy(way):
        return remote(
            link_out.at[way], link_in.at[way], link_sems, (way,), (s + (1 - 2 * way) * TEAM, g)
        )

    def arrive(way, there):
        @pl.when(there)
        def _():
            link_copy(way).wait_recv()

        return [jnp.where(there, link_in[way, h, 0:VARS, :], 0.0) for h in range(PAIR)]

    def depart(way, there, x):
        for h in range(PAIR):
            link_out[way, h, 0:VARS, :] = x[h]

        @pl.when(there)
        def _():
            link_copy(way).start()

    def upd_copy(k):
        q = lax.rem(place + k, TEAM)
        return remote(
            upd_out.at[q],
            upd_in.at[:, pl.ds(pl.multiple_of(place * PAIR * 8, PAIR * 8), PAIR * 8)],
            upd_sems,
            (k,),
            (base + q, g),
        )

    x = arrive(0, team > 0)
    stars = {}
    for k in range(TEAM):
        for r in range(ROWS):
            for h in range(PAIR):
                x[h] = offsets[k, r, h] + product(
                    lambda m: fmap[k, r, h, m, 0:VARS, :], x[h]
                )
                stars[k, r, h] = x[h]
    depart(0, team < n_teams - 1, x)
    x = arrive(1, team < n_teams - 1)
    for k in reversed(range(TEAM)):
        for r in reversed(range(ROWS)):
            for h in range(PAIR):
                x[h] = stars[k, r, h] + product(lambda m: bmap[k, r, h, m, 0:VARS, :], x[h])
                upd_out[k, r, h * 8 : h * 8 + VARS, :] = x[h]
    depart(1, team > 0, x)
    for k in range(1, TEAM):
        upd_copy(k).start()
    own = pltpu.make_async_copy(
        upd_out.at[place],
        upd_in.at[:, pl.ds(pl.multiple_of(place * PAIR * 8, PAIR * 8), PAIR * 8)],
        local_sems.at[2],
    )
    own.start()
    own.wait()
    for k in range(1, TEAM):
        q = lax.rem(place + TEAM - k, TEAM)
        pltpu.make_async_remote_copy(
            src_ref=upd_out.at[place],
            dst_ref=upd_in.at[:, pl.ds(pl.multiple_of(q * PAIR * 8, PAIR * 8), PAIR * 8)],
            send_sem=upd_sems.at[0, k],
            recv_sem=upd_sems.at[1, k],
            device_id=(base + lax.rem(place + k, TEAM), g),
            device_id_type=MESH,
        ).wait_recv()
    for r in range(ROWS):
        for v in range(VARS):
            at = (r * VARS + v) * 8
            new_state[at : at + 8, :] = current[at : at + 8, :] + upd_in[r, pl.ds(v, 8, stride=8), :]

    for k in range(1, TEAM):
        upd_copy(k).wait_send()
    for side in (0, 1):
        edge_copy(side).wait_send()
    for k in range(1, n_girth):
        packet_copy(0, k).wait_send()
    for ds in (-1, 1):

        @pl.when(has(ds))
        def _():
            row_copy((ds + 1) // 2).wait_send()
            for k in range(n_girth):
                packet_copy(ds, k).wait_send()

    for way, there in ((0, team < n_teams - 1), (1, team > 0)):

        @pl.when(there)
        def _():
            link_copy(way).wait_send()


def per_device(
    state,
    propeller,
    donor_index,
    fringe_index,
    donor_weight,
    disk_mask,
    thrust,
    face,
    coupling,
    diag_inverse,
    lower_jacobian,
    upper_jacobian,
):
    n_stream, n_girth = lax.axis_size("stream"), lax.axis_size("girth")
    f32 = jnp.float32
    vmem = pl.BlockSpec(memory_space=pltpu.VMEM)
    smem = pl.BlockSpec(memory_space=pltpu.SMEM)
    blocks = ROWS * VARS * 8
    padded = -(-ROWS * VARS * VARS // 8) * 8
    dma = pltpu.SemaphoreType.DMA
    new_state, residual = pl.pallas_call(
        functools.partial(kernel, n_stream, n_girth),
        out_shape=[jax.ShapeDtypeStruct((blocks, 128), f32)] * 2,
        in_specs=[vmem] * 6 + [smem, vmem, smem, vmem, smem, smem],
        out_specs=[vmem, vmem],
        scratch_shapes=[
            pltpu.VMEM((8, 128), f32),
            pltpu.VMEM((3, n_girth, 8, 128), f32),
            pltpu.VMEM((2, ROWS, 8, 128), f32),
            pltpu.VMEM((2, ROWS, 8, 128), f32),
            pltpu.VMEM((2, VARS * 8, 128), f32),
            pltpu.VMEM((padded * 8, 128), f32),
            pltpu.VMEM((TEAM, PAIR, padded, 128), f32),
            pltpu.VMEM((TEAM, PAIR, padded, 128), f32),
            pltpu.VMEM((blocks, 128), f32),
            pltpu.VMEM((ROWS, VARS * 8, 128), f32),
            pltpu.VMEM((TEAM, ROWS, PAIR, 8, 128), f32),
            pltpu.VMEM((TEAM, ROWS, PAIR, 8, 128), f32),
            pltpu.VMEM((TEAM, ROWS, PAIR, VARS, 8, 128), f32),
            pltpu.VMEM((TEAM, ROWS, PAIR, VARS, 8, 128), f32),
            pltpu.VMEM((TEAM, ROWS, PAIR * 8, 128), f32),
            pltpu.VMEM((ROWS, TEAM * PAIR * 8, 128), f32),
            pltpu.VMEM((2, PAIR, 8, 128), f32),
            pltpu.VMEM((2, PAIR, 8, 128), f32),
            dma((2, 3, n_girth)),
            dma((2, 2)),
            dma((2, 2)),
            dma((2, TEAM)),
            dma((2, TEAM)),
            dma((2, TEAM)),
            dma((2, 2)),
            dma((3,)),
        ],
        compiler_params=pltpu.CompilerParams(
            collective_id=0, has_side_effects=True, vmem_limit_bytes=24 * 1024 * 1024
        ),
        cost_estimate=pl.CostEstimate(flops=12_000_000, bytes_accessed=500_000, transcendentals=0),
    )(
        state.reshape(blocks, 128),
        propeller,
        donor_index,
        fringe_index,
        donor_weight,
        disk_mask.reshape(ROWS * 8, 128),
        thrust,
        face.reshape(ROWS * 6 * 8, 128),
        coupling,
        diag_inverse,
        lower_jacobian,
        upper_jacobian,
    )
    return new_state.reshape(state.shape), residual.reshape(state.shape)


def solution(mesh):
    placed = (
        P("stream", None, "girth", None),
        P(None, ("stream", "girth")),
        P(("stream", "girth"), None),
        P(("stream", "girth"), None),
        P(("stream", "girth"), None),
        P("stream", "girth", None),
        P(),
        P("stream", None, "girth", None),
        P(),
        P("stream", None, None, "girth", None),
        P(),
        P(),
    )
    return jax.shard_map(
        per_device,
        mesh=mesh,
        in_specs=placed,
        out_specs=(P("stream", None, "girth", None), P("stream", None, "girth", None)),
        check_vma=False,
    )
```

```python
import functools

import jax
import jax.numpy as jnp
from jax import lax
from jax.experimental import pallas as pl
from jax.experimental.pallas import tpu as pltpu
from jax.sharding import PartitionSpec as P

MESH = pl.DeviceIdType.MESH
PRECISE = lax.Precision.HIGHEST
VARS = 7
ROWS = 2
TEAM = 4
PAIR = 2
CAP = 8


def kernel(
    n_stream,
    n_girth,
    *refs,
):
    given, results, held = refs[:12], refs[12:14], refs[14:26]
    state, prop, donor, landing, weight, disk = held[:6]
    thrust, face, coupling, inverse, lower, upper = held[6:]
    (
        new_state,
        residual_out,
        packet,
        packets,
        edge_out,
        edge_in,
        row_in,
        planes,
        inv_out,
        inv_in,
        current,
        rhs_planes,
        rhs_out,
        rhs_in,
        fmap,
        bmap,
        upd_out,
        upd_in,
        link_out,
        link_in,
        packet_sems,
        edge_sems,
        row_sems,
        inv_sems,
        rhs_sems,
        upd_sems,
        link_sems,
        local_sems,
        load_sems,
        store_sems,
    ) = refs[26:]
    s, g = lax.axis_index("stream"), lax.axis_index("girth")
    base = (s // TEAM) * TEAM
    place = s - base
    team = s // TEAM
    n_teams = n_stream // TEAM
    slots = donor.shape[1]
    packs = n_girth if n_girth * slots <= 128 else 1

    def girth_at(k):
        return lax.rem(g + k + n_girth, n_girth)

    def remote(src, dst, sems, at, to):
        return pltpu.make_async_remote_copy(
            src_ref=src,
            dst_ref=dst,
            send_sem=sems.at[(0, *at)],
            recv_sem=sems.at[(1, *at)],
            device_id=to,
            device_id_type=MESH,
        )

    def has(ds):
        return jnp.logical_and(s + ds >= 0, s + ds < n_stream)

    def load(n):
        return pltpu.make_async_copy(given[n], held[n], load_sems.at[n])

    for n in (2, 3, 4, 1, 0, 9, 7, 8, 5, 6, 10, 11):
        load(n).start()

    barrier = pltpu.get_barrier_semaphore()

    def greet(to):
        pl.semaphore_signal(barrier, inc=1, device_id=to, device_id_type=MESH)

    for k in range(1, n_girth):
        greet((s, girth_at(k)))
    expected = n_girth - 1
    for ds in (-1, 1):

        @pl.when(has(ds))
        def _():
            for k in range(n_girth):
                greet((s + ds, girth_at(k)))

        expected = expected + jnp.where(has(ds), n_girth, 0)
    for k in range(1, TEAM):
        q = lax.rem(place + k, TEAM)
        far = jnp.logical_or(q - place > 1, place - q > 1)

        @pl.when(far)
        def _():
            greet((base + q, g))

        expected = expected + jnp.where(far, 1, 0)
    for ds in (-TEAM, TEAM):

        @pl.when(has(ds))
        def _():
            greet((s + ds, g))

        expected = expected + jnp.where(has(ds), 1, 0)

    for n in (1, 2, 3, 4):
        load(n).wait()

    lane = lax.broadcasted_iota(jnp.int32, (1, 128), 1)

    def spread(ref):
        return jnp.concatenate([ref[...]] * packs, axis=1) if packs > 1 else ref[...]

    donor_all = spread(donor)
    live = jnp.logical_and(lane // slots == lax.rem(g, packs), donor_all >= 0)
    cell = lax.broadcasted_iota(jnp.int32, (prop.shape[1], 128), 0)
    chosen = jnp.where(cell == jnp.where(live, donor_all, -1), 1.0, 0.0)
    taken = jnp.dot(prop[...], chosen, precision=PRECISE, preferred_element_type=jnp.float32)
    packet[0:VARS, :] = taken * jnp.where(live, spread(weight), 0.0)
    packet[VARS : VARS + 1, :] = jnp.where(live, spread(landing) + 1, 0).astype(jnp.float32)
    packets[1, 0] = packet[...]

    load(0).wait()
    for side, at in ((0, 0), (1, 7)):
        for r in range(ROWS):
            edge_out[side, r, 0:VARS, :] = state[pl.ds(r * VARS * 8 + at, VARS, stride=8), :]
            edge_out[side, r, VARS : VARS + 1, :] = jnp.zeros((1, 128), jnp.float32)

    load(9).wait()
    for r in range(ROWS):
        for i in range(VARS):
            for j in range(VARS):
                p = (r * VARS + i) * VARS + j
                planes[p * 8 : p * 8 + 8, :] = inverse[r, i, j].astype(jnp.float32)
    blocks = planes.shape[0] // 64
    planes[ROWS * VARS * VARS * 8 :, :] = jnp.zeros(
        (planes.shape[0] - ROWS * VARS * VARS * 8, 128), jnp.float32
    )
    for c in range(8):
        for b in range(blocks):
            inv_out[c // PAIR, c % PAIR, b * 8 : b * 8 + 8, :] = planes[
                pl.ds(b * 64 + c, 8, stride=8), :
            ]

    pl.semaphore_wait(barrier, expected)

    def packet_copy(ds, k):
        return remote(
            packet, packets.at[1 - ds, k], packet_sems, (1 - ds, k), (s + ds, girth_at(k))
        )

    def edge_copy(side):
        return remote(
            edge_out.at[side], edge_in.at[side], edge_sems, (side,), (s, girth_at(2 * side - 1))
        )

    def row_copy(side):
        rows = VARS * 8
        return remote(
            state.at[pl.ds(side * rows, rows)],
            row_in.at[side],
            row_sems,
            (side,),
            (s + 2 * side - 1, g),
        )

    for ds in (-1, 1):

        @pl.when(has(ds))
        def _():
            row_copy((ds + 1) // 2).start()
            for k in range(n_girth):
                packet_copy(ds, k).start()

    for side in (0, 1):
        edge_copy(side).start()
    for k in range(1, n_girth):
        packet_copy(0, k).start()

    def team_copy(out, into, sems, k):
        q = lax.rem(place + k, TEAM)
        return remote(out.at[q], into.at[place], sems, (k,), (base + q, g))

    def own_copy(out, into, n):
        return pltpu.make_async_copy(out.at[place], into.at[place], local_sems.at[n])

    for k in range(1, TEAM):
        team_copy(inv_out, inv_in, inv_sems, k).start()
    own_copy(inv_out, inv_in, 0).start()

    for side in (0, 1):
        edge_copy(side).wait_recv()
    for k in range(1, n_girth):
        packet_copy(0, k).wait_recv()
    for ds in (-1, 1):

        @pl.when(has(ds))
        def _():
            row_copy((1 - ds) // 2).wait_recv()
            for k in range(n_girth):
                packet_copy(-ds, k).wait_recv()

    girth_cell = lax.broadcasted_iota(jnp.int32, (8, 128), 0)
    normal_cell = lax.broadcasted_iota(jnp.int32, (8, 128), 1)
    normal_rows = lax.broadcasted_iota(jnp.int32, (128, 128), 0)
    var_row = lax.broadcasted_iota(jnp.int32, (8, 128), 0)
    peer = lax.rem(lane, slots) // CAP

    def landed(o, plan):
        total = None
        for first in range(0, n_girth, packs):
            tile = packets[o, first]
            for k in range(first + 1, first + packs):
                tile = tile + packets[o, k]
            code = tile[VARS : VARS + 1, :].astype(jnp.int32) - 1
            row, gc, nc = code >> 10, (code >> 7) & 7, code & 127
            nc = jnp.where(code >= 0, nc, -1)
            tile = jnp.where(var_row == VARS, 1.0, tile)
            part = lax.dot_general(
                jnp.concatenate(plan(tile, row, gc), axis=0),
                jnp.where(normal_rows == nc, 1.0, 0.0),
                (((1,), (1,)), ((), ())),
                precision=PRECISE,
                preferred_element_type=jnp.float32,
            )
            total = part if total is None else total + part
        return total

    def block_rows(r):
        def plan(tile, row, gc):
            here = jnp.logical_and(row == r, peer == g)
            hit = jnp.where(girth_cell == jnp.where(here, gc, -1), 1.0, 0.0)
            return [tile[v : v + 1, :] * hit for v in range(8)]

        return plan

    def own_plan(tile, row, gc):
        rows = block_rows(0)(tile, row, gc) + block_rows(1)(tile, row, gc)
        for at, side in ((7, -1), (0, 1)):
            for r in range(ROWS):
                here = (peer == girth_at(side)) & (row == r) & (gc == at)
                rows.append(tile * jnp.where(here, 1.0, 0.0))
        return rows

    def settle(found, raw):
        hit = found[VARS * 8 : VARS * 8 + 8] > 0.5
        return [jnp.where(hit, found[v * 8 : v * 8 + 8], raw(v)) for v in range(VARS)], hit

    own = landed(1, own_plan)
    cells, fringe = [], []
    for r in range(ROWS):
        found, hit = settle(
            own[r * 64 : r * 64 + 64], lambda v: state[(r * VARS + v) * 8 : (r * VARS + v) * 8 + 8, :]
        )
        cells.append(found)
        fringe.append(hit)
        for v in range(VARS):
            current[(r * VARS + v) * 8 : (r * VARS + v) * 8 + 8, :] = found[v]
    beside = {}
    for side in (0, 1):
        for r in range(ROWS):
            at = 128 + (side * ROWS + r) * 8
            found = own[at : at + 8]
            beside[side, r] = jnp.where(
                found[VARS : VARS + 1] > 0.5, found, edge_in[1 - side, r]
            )
    outer = []
    for o, r, side in ((0, 1, 1), (2, 0, 0)):
        found, _ = settle(
            landed(o, block_rows(r)), lambda v: row_in[side, v * 8 : v * 8 + 8, :]
        )
        outer.append([jnp.where(has(o - 1), x, 0.0) for x in found])

    for n in (5, 6, 7, 8, 10, 11):
        load(n).wait()
    for r in range(ROWS):
        here = cells[r]
        before = outer[0] if r == 0 else cells[r - 1]
        after = outer[1] if r == ROWS - 1 else cells[r + 1]
        in_disk = disk[r * 8 : r * 8 + 8, :].astype(jnp.float32)
        total = [in_disk * thrust[v] for v in range(VARS)]
        for d in range(6):
            step = []
            for v in range(VARS):
                x = here[v]
                if d == 0:
                    near = before[v]
                elif d == 1:
                    near = after[v]
                elif d == 2:
                    near = jnp.where(girth_cell == 0, beside[0, r][v : v + 1], pltpu.roll(x, 1, 0))
                elif d == 3:
                    near = jnp.where(girth_cell == 7, beside[1, r][v : v + 1], pltpu.roll(x, 7, 0))
                elif d == 4:
                    near = jnp.where(normal_cell == 0, 0.0, pltpu.roll(x, 1, 1))
                else:
                    near = jnp.where(normal_cell == 127, 0.0, pltpu.roll(x, 127, 1))
                step.append(near - x)
            area = face[(r * 6 + d) * 8 : (r * 6 + d) * 8 + 8, :]
            for i in range(VARS):
                flux = step[0] * coupling[d, i, 0]
                for j in range(1, VARS):
                    flux = flux + step[j] * coupling[d, i, j]
                total[i] = total[i] + area * flux
        for v in range(VARS):
            residual_out[(r * VARS + v) * 8 : (r * VARS + v) * 8 + 8, :] = total[v]
            rhs_planes[r, v * 8 : v * 8 + 8, :] = jnp.where(fringe[r], 0.0, -total[v])
        for c in range(8):
            rhs_out[c // PAIR, r, c % PAIR, 0:VARS, :] = rhs_planes[r, pl.ds(c, VARS, stride=8), :]

    for k in range(1, TEAM):
        team_copy(rhs_out, rhs_in, rhs_sems, k).start()
    own_copy(rhs_out, rhs_in, 1).start()
    keep = [
        pltpu.make_async_copy(new_state, results[0], store_sems.at[0]),
        pltpu.make_async_copy(residual_out, results[1], store_sems.at[1]),
    ]
    keep[1].start()

    for k in range(1, TEAM):
        team_copy(inv_out, inv_in, inv_sems, TEAM - k).wait_send()
        pltpu.make_async_remote_copy(
            src_ref=inv_out.at[place],
            dst_ref=inv_in.at[lax.rem(place + TEAM - k, TEAM)],
            send_sem=inv_sems.at[0, k],
            recv_sem=inv_sems.at[1, k],
            device_id=(base + lax.rem(place + k, TEAM), g),
            device_id_type=MESH,
        ).wait_recv()
    own_copy(inv_out, inv_in, 0).wait()

    def column(k, h, r, j):
        return inv_in[k, h, pl.ds(r * VARS * VARS + j, VARS, stride=VARS), :]

    def matrices(k, carry):
        for r in range(ROWS):
            for h in range(PAIR):
                cols = [column(k, h, r, j) for j in range(VARS)]
                for m in range(VARS):
                    f, b = cols[0] * lower[0, m], cols[0] * upper[0, m]
                    for j in range(1, VARS):
                        f = f + cols[j] * lower[j, m]
                        b = b + cols[j] * upper[j, m]
                    fmap[k, r, h, m, 0:VARS, :] = f
                    bmap[k, r, h, m, 0:VARS, :] = b
        return carry

    lax.fori_loop(0, TEAM, matrices, 0)

    for k in range(1, TEAM):
        team_copy(rhs_out, rhs_in, rhs_sems, TEAM - k).wait_send()
        pltpu.make_async_remote_copy(
            src_ref=rhs_out.at[place],
            dst_ref=rhs_in.at[lax.rem(place + TEAM - k, TEAM)],
            send_sem=rhs_sems.at[0, k],
            recv_sem=rhs_sems.at[1, k],
            device_id=(base + lax.rem(place + k, TEAM), g),
            device_id_type=MESH,
        ).wait_recv()
    own_copy(rhs_out, rhs_in, 1).wait()

    def product(matrix, x):
        parts = [matrix(j) * x[j : j + 1, :] for j in range(VARS)]
        return ((parts[0] + parts[1]) + (parts[2] + parts[3])) + (
            (parts[4] + parts[5]) + parts[6]
        )

    offsets = {}
    for k in range(TEAM):
        for r in range(ROWS):
            for h in range(PAIR):
                offsets[k, r, h] = product(
                    lambda j: column(k, h, r, j), rhs_in[k, r, h, 0:VARS, :]
                )

    def link_copy(way):
        return remote(
            link_out.at[way], link_in.at[way], link_sems, (way,), (s + (1 - 2 * way) * TEAM, g)
        )

    def arrive(way, there):
        @pl.when(there)
        def _():
            link_copy(way).wait_recv()

        return [jnp.where(there, link_in[way, h, 0:VARS, :], 0.0) for h in range(PAIR)]

    def depart(way, there, x):
        for h in range(PAIR):
            link_out[way, h, 0:VARS, :] = x[h]

        @pl.when(there)
        def _():
            link_copy(way).start()

    def upd_copy(k):
        q = lax.rem(place + k, TEAM)
        return remote(
            upd_out.at[q],
            upd_in.at[:, pl.ds(pl.multiple_of(place * PAIR * 8, PAIR * 8), PAIR * 8)],
            upd_sems,
            (k,),
            (base + q, g),
        )

    x = arrive(0, team > 0)
    stars = {}
    for k in range(TEAM):
        for r in range(ROWS):
            for h in range(PAIR):
                x[h] = offsets[k, r, h] + product(
                    lambda m: fmap[k, r, h, m, 0:VARS, :], x[h]
                )
                stars[k, r, h] = x[h]
    depart(0, team < n_teams - 1, x)
    x = arrive(1, team < n_teams - 1)
    for k in reversed(range(TEAM)):
        for r in reversed(range(ROWS)):
            for h in range(PAIR):
                x[h] = stars[k, r, h] + product(lambda m: bmap[k, r, h, m, 0:VARS, :], x[h])
                upd_out[k, r, h * 8 : h * 8 + VARS, :] = x[h]
    depart(1, team > 0, x)
    for k in range(1, TEAM):
        upd_copy(k).start()
    own = pltpu.make_async_copy(
        upd_out.at[place],
        upd_in.at[:, pl.ds(pl.multiple_of(place * PAIR * 8, PAIR * 8), PAIR * 8)],
        local_sems.at[2],
    )
    own.start()
    own.wait()
    for k in range(1, TEAM):
        q = lax.rem(place + TEAM - k, TEAM)
        pltpu.make_async_remote_copy(
            src_ref=upd_out.at[place],
            dst_ref=upd_in.at[:, pl.ds(pl.multiple_of(q * PAIR * 8, PAIR * 8), PAIR * 8)],
            send_sem=upd_sems.at[0, k],
            recv_sem=upd_sems.at[1, k],
            device_id=(base + lax.rem(place + k, TEAM), g),
            device_id_type=MESH,
        ).wait_recv()
    for r in range(ROWS):
        for v in range(VARS):
            at = (r * VARS + v) * 8
            new_state[at : at + 8, :] = current[at : at + 8, :] + upd_in[r, pl.ds(v, 8, stride=8), :]

    keep[0].start()

    for k in range(1, TEAM):
        upd_copy(k).wait_send()
    for side in (0, 1):
        edge_copy(side).wait_send()
    for k in range(1, n_girth):
        packet_copy(0, k).wait_send()
    for ds in (-1, 1):

        @pl.when(has(ds))
        def _():
            row_copy((ds + 1) // 2).wait_send()
            for k in range(n_girth):
                packet_copy(ds, k).wait_send()

    for way, there in ((0, team < n_teams - 1), (1, team > 0)):

        @pl.when(there)
        def _():
            link_copy(way).wait_send()

    for copy in keep:
        copy.wait()


def store(a, b, a_out, b_out, sems):
    copies = [
        pltpu.make_async_copy(a, a_out, sems.at[0]),
        pltpu.make_async_copy(b, b_out, sems.at[1]),
    ]
    for copy in copies:
        copy.start()
    for copy in copies:
        copy.wait()


def per_device(
    state,
    propeller,
    donor_index,
    fringe_index,
    donor_weight,
    disk_mask,
    thrust,
    face,
    coupling,
    diag_inverse,
    lower_jacobian,
    upper_jacobian,
):
    n_stream, n_girth = lax.axis_size("stream"), lax.axis_size("girth")
    f32 = jnp.float32
    hbm = pl.BlockSpec(memory_space=pltpu.HBM)
    blocks = ROWS * VARS * 8
    padded = -(-ROWS * VARS * VARS // 8) * 8
    dma = pltpu.SemaphoreType.DMA
    given = (
        state.reshape(blocks, 128),
        propeller,
        donor_index,
        fringe_index,
        donor_weight,
        disk_mask.reshape(ROWS * 8, 128),
        thrust,
        face.reshape(ROWS * 6 * 8, 128),
        coupling,
        diag_inverse,
        lower_jacobian,
        upper_jacobian,
    )
    scalars = (6, 8, 10, 11)
    held = [
        (pltpu.SMEM if n in scalars else pltpu.VMEM)(x.shape, x.dtype) for n, x in enumerate(given)
    ]
    results = [jax.ShapeDtypeStruct((blocks, 128), f32)] * 2
    new_state, residual = pl.pallas_call(
        functools.partial(kernel, n_stream, n_girth),
        out_shape=results,
        in_specs=[hbm] * 12,
        out_specs=[hbm, hbm],
        scratch_shapes=held
        + [
            pltpu.VMEM((blocks, 128), f32),
            pltpu.VMEM((blocks, 128), f32),
            pltpu.VMEM((8, 128), f32),
            pltpu.VMEM((3, n_girth, 8, 128), f32),
            pltpu.VMEM((2, ROWS, 8, 128), f32),
            pltpu.VMEM((2, ROWS, 8, 128), f32),
            pltpu.VMEM((2, VARS * 8, 128), f32),
            pltpu.VMEM((padded * 8, 128), f32),
            pltpu.VMEM((TEAM, PAIR, padded, 128), f32),
            pltpu.VMEM((TEAM, PAIR, padded, 128), f32),
            pltpu.VMEM((blocks, 128), f32),
            pltpu.VMEM((ROWS, VARS * 8, 128), f32),
            pltpu.VMEM((TEAM, ROWS, PAIR, 8, 128), f32),
            pltpu.VMEM((TEAM, ROWS, PAIR, 8, 128), f32),
            pltpu.VMEM((TEAM, ROWS, PAIR, VARS, 8, 128), f32),
            pltpu.VMEM((TEAM, ROWS, PAIR, VARS, 8, 128), f32),
            pltpu.VMEM((TEAM, ROWS, PAIR * 8, 128), f32),
            pltpu.VMEM((ROWS, TEAM * PAIR * 8, 128), f32),
            pltpu.VMEM((2, PAIR, 8, 128), f32),
            pltpu.VMEM((2, PAIR, 8, 128), f32),
            dma((2, 3, n_girth)),
            dma((2, 2)),
            dma((2, 2)),
            dma((2, TEAM)),
            dma((2, TEAM)),
            dma((2, TEAM)),
            dma((2, 2)),
            dma((3,)),
            dma((12,)),
            dma((2,)),
        ],
        compiler_params=pltpu.CompilerParams(
            collective_id=0, has_side_effects=True, vmem_limit_bytes=60 * 1024 * 1024
        ),
        cost_estimate=pl.CostEstimate(flops=12_000_000, bytes_accessed=500_000, transcendentals=0),
    )(*given)
    new_state, residual = pl.pallas_call(
        store,
        out_shape=results,
        in_specs=[hbm, hbm],
        out_specs=[hbm, hbm],
        scratch_shapes=[dma((2,))],
        compiler_params=pltpu.CompilerParams(vmem_limit_bytes=60 * 1024 * 1024),
    )(new_state, residual)
    return new_state.reshape(state.shape), residual.reshape(state.shape)


def solution(mesh):
    placed = (
        P("stream", None, "girth", None),
        P(None, ("stream", "girth")),
        P(("stream", "girth"), None),
        P(("stream", "girth"), None),
        P(("stream", "girth"), None),
        P("stream", "girth", None),
        P(),
        P("stream", None, "girth", None),
        P(),
        P("stream", None, None, "girth", None),
        P(),
        P(),
    )
    return jax.shard_map(
        per_device,
        mesh=mesh,
        in_specs=placed,
        out_specs=(P("stream", None, "girth", None), P("stream", None, "girth", None)),
        check_vma=False,
    )
```

```python
import functools

import jax
import jax.numpy as jnp
from jax import lax
from jax.experimental import pallas as pl
from jax.experimental.pallas import tpu as pltpu
from jax.sharding import PartitionSpec as P

MESH = pl.DeviceIdType.MESH
PRECISE = lax.Precision.HIGHEST
VARS = 7
ROWS = 2
TEAM = 4
PAIR = 2
CAP = 8


def kernel(
    n_stream,
    n_girth,
    *refs,
):
    given, results, held = refs[:12], refs[12:14], refs[14:26]
    state, prop, donor, landing, weight, disk = held[:6]
    thrust, face, coupling, inverse, lower, upper = held[6:]
    (
        new_state,
        residual_out,
        packet,
        packets,
        edge_out,
        edge_in,
        row_out,
        row_in,
        planes,
        inv_out,
        inv_in,
        current,
        rhs_planes,
        rhs_out,
        rhs_in,
        fmap,
        bmap,
        upd_out,
        upd_in,
        link_out,
        link_in,
        packet_sems,
        edge_sems,
        row_sems,
        inv_sems,
        rhs_sems,
        upd_sems,
        link_sems,
        local_sems,
        load_sems,
        store_sems,
    ) = refs[26:]
    s, g = lax.axis_index("stream"), lax.axis_index("girth")
    base = (s // TEAM) * TEAM
    place = s - base
    team = s // TEAM
    n_teams = n_stream // TEAM
    slots = donor.shape[1]
    packs = n_girth if n_girth * slots <= 128 else 1

    def girth_at(k):
        return lax.rem(g + k + n_girth, n_girth)

    def remote(src, dst, sems, at, to):
        return pltpu.make_async_remote_copy(
            src_ref=src,
            dst_ref=dst,
            send_sem=sems.at[(0, *at)],
            recv_sem=sems.at[(1, *at)],
            device_id=to,
            device_id_type=MESH,
        )

    def has(ds):
        return jnp.logical_and(s + ds >= 0, s + ds < n_stream)

    def load(n):
        return pltpu.make_async_copy(given[n], held[n], load_sems.at[n])

    for n in (2, 3, 4, 1, 0, 9, 7, 8, 5, 6, 10, 11):
        load(n).start()

    barrier = pltpu.get_barrier_semaphore()

    def greet(to):
        pl.semaphore_signal(barrier, inc=1, device_id=to, device_id_type=MESH)

    for k in range(1, n_girth):
        greet((s, girth_at(k)))
    expected = n_girth - 1
    for ds in (-1, 1):

        @pl.when(has(ds))
        def _():
            for k in range(n_girth):
                greet((s + ds, girth_at(k)))

        expected = expected + jnp.where(has(ds), n_girth, 0)
    for k in range(1, TEAM):
        q = lax.rem(place + k, TEAM)
        far = jnp.logical_or(q - place > 1, place - q > 1)

        @pl.when(far)
        def _():
            greet((base + q, g))

        expected = expected + jnp.where(far, 1, 0)
    for ds in (-TEAM, TEAM):

        @pl.when(has(ds))
        def _():
            greet((s + ds, g))

        expected = expected + jnp.where(has(ds), 1, 0)

    for n in (1, 2, 3, 4):
        load(n).wait()

    lane = lax.broadcasted_iota(jnp.int32, (1, 128), 1)

    def spread(ref):
        return jnp.concatenate([ref[...]] * packs, axis=1) if packs > 1 else ref[...]

    donor_all = spread(donor)
    live = jnp.logical_and(lane // slots == lax.rem(g, packs), donor_all >= 0)
    cell = lax.broadcasted_iota(jnp.int32, (prop.shape[1], 128), 0)
    chosen = jnp.where(cell == jnp.where(live, donor_all, -1), 1.0, 0.0)
    taken = jnp.dot(prop[...], chosen, precision=PRECISE, preferred_element_type=jnp.float32)
    packet[0:VARS, :] = taken * jnp.where(live, spread(weight), 0.0)
    packet[VARS : VARS + 1, :] = jnp.where(live, spread(landing) + 1, 0).astype(jnp.float32)

    load(0).wait()
    for side, at in ((0, 0), (1, 7)):
        for r in range(ROWS):
            edge_out[side, r, 0:VARS, :] = state[pl.ds(r * VARS * 8 + at, VARS, stride=8), :]
            edge_out[side, r, VARS : VARS + 1, :] = jnp.zeros((1, 128), jnp.float32)
        edge_out[side, ROWS] = packet[...]
        row_out[side, 0 : VARS * 8, :] = state[
            side * (ROWS - 1) * VARS * 8 : (side * (ROWS - 1) + 1) * VARS * 8, :
        ]
        row_out[side, VARS * 8 :, :] = packet[...]

    load(9).wait()
    for r in range(ROWS):
        for i in range(VARS):
            for j in range(VARS):
                p = (r * VARS + i) * VARS + j
                planes[p * 8 : p * 8 + 8, :] = inverse[r, i, j].astype(jnp.float32)
    blocks = planes.shape[0] // 64
    planes[ROWS * VARS * VARS * 8 :, :] = jnp.zeros(
        (planes.shape[0] - ROWS * VARS * VARS * 8, 128), jnp.float32
    )
    for c in range(8):
        for b in range(blocks):
            inv_out[c // PAIR, c % PAIR, b * 8 : b * 8 + 8, :] = planes[
                pl.ds(b * 64 + c, 8, stride=8), :
            ]

    pl.semaphore_wait(barrier, expected)

    def packet_copy(ds, k):
        return remote(
            packet, packets.at[1 - ds, k], packet_sems, (1 - ds, k), (s + ds, girth_at(k))
        )

    def edge_copy(side):
        return remote(
            edge_out.at[side], edge_in.at[side], edge_sems, (side,), (s, girth_at(2 * side - 1))
        )

    def row_copy(side):
        return remote(
            row_out.at[side],
            row_in.at[side],
            row_sems,
            (side,),
            (s + 2 * side - 1, g),
        )

    for ds in (-1, 1):

        @pl.when(has(ds))
        def _():
            row_copy((ds + 1) // 2).start()
            for k in range(1, n_girth):
                packet_copy(ds, k).start()

    for side in (0, 1):
        edge_copy(side).start()
    for k in range(2, n_girth - 1):
        packet_copy(0, k).start()

    def team_copy(out, into, sems, k):
        q = lax.rem(place + k, TEAM)
        return remote(out.at[q], into.at[place], sems, (k,), (base + q, g))

    def team_arrival(out, into, sems, k):
        return pltpu.make_async_remote_copy(
            src_ref=out.at[place],
            dst_ref=into.at[lax.rem(place + TEAM - k, TEAM)],
            send_sem=sems.at[0, k],
            recv_sem=sems.at[1, k],
            device_id=(base + lax.rem(place + k, TEAM), g),
            device_id_type=MESH,
        )

    far_first = sorted(range(1, TEAM), key=lambda k: -min(k, TEAM - k))

    def own_copy(out, into, n):
        return pltpu.make_async_copy(out.at[place], into.at[place], local_sems.at[n])

    for k in far_first:
        team_copy(inv_out, inv_in, inv_sems, k).start()
    own_copy(inv_out, inv_in, 0).start()

    for side in (0, 1):
        edge_copy(side).wait_recv()
    for k in range(2, n_girth - 1):
        packet_copy(0, k).wait_recv()
    for ds in (-1, 1):

        @pl.when(has(ds))
        def _():
            row_copy((1 - ds) // 2).wait_recv()
            for k in range(1, n_girth):
                packet_copy(-ds, k).wait_recv()

    girth_cell = lax.broadcasted_iota(jnp.int32, (8, 128), 0)
    normal_cell = lax.broadcasted_iota(jnp.int32, (8, 128), 1)
    normal_rows = lax.broadcasted_iota(jnp.int32, (128, 128), 0)
    var_row = lax.broadcasted_iota(jnp.int32, (8, 128), 0)
    peer = lax.rem(lane, slots) // CAP

    def packet_from(o, k):
        if o != 1 and k == 0:
            return row_in[1 - o // 2, VARS * 8 :, :]
        if o == 1 and k in (1, n_girth - 1):
            return edge_in[1 if k == 1 else 0, ROWS]
        return packet[...] if k == 0 else packets[o, k]

    def landed(o, plan):
        total = None
        for first in range(0, n_girth, packs):
            tile = packet_from(o, first)
            for k in range(first + 1, first + packs):
                tile = tile + packet_from(o, k)
            code = tile[VARS : VARS + 1, :].astype(jnp.int32) - 1
            row, gc, nc = code >> 10, (code >> 7) & 7, code & 127
            nc = jnp.where(code >= 0, nc, -1)
            tile = jnp.where(var_row == VARS, 1.0, tile)
            part = lax.dot_general(
                jnp.concatenate(plan(tile, row, gc), axis=0),
                jnp.where(normal_rows == nc, 1.0, 0.0),
                (((1,), (1,)), ((), ())),
                precision=PRECISE,
                preferred_element_type=jnp.float32,
            )
            total = part if total is None else total + part
        return total

    def block_rows(r):
        def plan(tile, row, gc):
            here = jnp.logical_and(row == r, peer == g)
            hit = jnp.where(girth_cell == jnp.where(here, gc, -1), 1.0, 0.0)
            return [tile[v : v + 1, :] * hit for v in range(8)]

        return plan

    def own_plan(tile, row, gc):
        rows = block_rows(0)(tile, row, gc) + block_rows(1)(tile, row, gc)
        for at, side in ((7, -1), (0, 1)):
            for r in range(ROWS):
                here = (peer == girth_at(side)) & (row == r) & (gc == at)
                rows.append(tile * jnp.where(here, 1.0, 0.0))
        return rows

    def settle(found, raw):
        hit = found[VARS * 8 : VARS * 8 + 8] > 0.5
        return [jnp.where(hit, found[v * 8 : v * 8 + 8], raw(v)) for v in range(VARS)], hit

    own = landed(1, own_plan)
    cells, fringe = [], []
    for r in range(ROWS):
        found, hit = settle(
            own[r * 64 : r * 64 + 64], lambda v: state[(r * VARS + v) * 8 : (r * VARS + v) * 8 + 8, :]
        )
        cells.append(found)
        fringe.append(hit)
        for v in range(VARS):
            current[(r * VARS + v) * 8 : (r * VARS + v) * 8 + 8, :] = found[v]
    beside = {}
    for side in (0, 1):
        for r in range(ROWS):
            at = 128 + (side * ROWS + r) * 8
            found = own[at : at + 8]
            beside[side, r] = jnp.where(
                found[VARS : VARS + 1] > 0.5, found, edge_in[1 - side, r]
            )
    outer = []
    for o, r, side in ((0, 1, 1), (2, 0, 0)):
        found, _ = settle(
            landed(o, block_rows(r)), lambda v: row_in[side, v * 8 : v * 8 + 8, :]
        )
        outer.append([jnp.where(has(o - 1), x, 0.0) for x in found])

    for n in (5, 6, 7, 8, 10, 11):
        load(n).wait()
    for r in range(ROWS):
        here = cells[r]
        before = outer[0] if r == 0 else cells[r - 1]
        after = outer[1] if r == ROWS - 1 else cells[r + 1]
        in_disk = disk[r * 8 : r * 8 + 8, :].astype(jnp.float32)
        total = [in_disk * thrust[v] for v in range(VARS)]
        for d in range(6):
            step = []
            for v in range(VARS):
                x = here[v]
                if d == 0:
                    near = before[v]
                elif d == 1:
                    near = after[v]
                elif d == 2:
                    near = jnp.where(girth_cell == 0, beside[0, r][v : v + 1], pltpu.roll(x, 1, 0))
                elif d == 3:
                    near = jnp.where(girth_cell == 7, beside[1, r][v : v + 1], pltpu.roll(x, 7, 0))
                elif d == 4:
                    near = jnp.where(normal_cell == 0, 0.0, pltpu.roll(x, 1, 1))
                else:
                    near = jnp.where(normal_cell == 127, 0.0, pltpu.roll(x, 127, 1))
                step.append(near - x)
            area = face[(r * 6 + d) * 8 : (r * 6 + d) * 8 + 8, :]
            for i in range(VARS):
                flux = step[0] * coupling[d, i, 0]
                for j in range(1, VARS):
                    flux = flux + step[j] * coupling[d, i, j]
                total[i] = total[i] + area * flux
        for v in range(VARS):
            residual_out[(r * VARS + v) * 8 : (r * VARS + v) * 8 + 8, :] = total[v]
            rhs_planes[r, v * 8 : v * 8 + 8, :] = jnp.where(fringe[r], 0.0, -total[v])
        for c in range(8):
            rhs_out[c // PAIR, r, c % PAIR, 0:VARS, :] = rhs_planes[r, pl.ds(c, VARS, stride=8), :]

    for k in far_first:
        team_copy(rhs_out, rhs_in, rhs_sems, k).start()
    own_copy(rhs_out, rhs_in, 1).start()
    keep = [
        pltpu.make_async_copy(new_state, results[0], store_sems.at[0]),
        pltpu.make_async_copy(residual_out, results[1], store_sems.at[1]),
    ]
    keep[1].start()

    def column(k, h, r, j):
        return inv_in[k, h, pl.ds(r * VARS * VARS + j, VARS, stride=VARS), :]

    def matrices(k):
        for r in range(ROWS):
            for h in range(PAIR):
                cols = [column(k, h, r, j) for j in range(VARS)]
                for m in range(VARS):
                    f, b = cols[0] * lower[0, m], cols[0] * upper[0, m]
                    for j in range(1, VARS):
                        f = f + cols[j] * lower[j, m]
                        b = b + cols[j] * upper[j, m]
                    fmap[k, r, h, m, 0:VARS, :] = f
                    bmap[k, r, h, m, 0:VARS, :] = b

    def arrived(step):
        @pl.when(step == 0)
        def _():
            own_copy(inv_out, inv_in, 0).wait()

        for n, k in enumerate(reversed(far_first)):

            @pl.when(step == n + 1)
            def _():
                team_arrival(inv_out, inv_in, inv_sems, k).wait()

    def take_blocks(step, carry):
        arrived(step)
        away = (step + 1) // 2 * (2 * lax.rem(step + 1, 2) - 1)
        matrices(lax.rem(place - away + TEAM, TEAM))
        return carry

    lax.fori_loop(0, TEAM, take_blocks, 0)

    for k in range(1, TEAM):
        team_arrival(rhs_out, rhs_in, rhs_sems, k).wait()
    own_copy(rhs_out, rhs_in, 1).wait()

    def product(matrix, x):
        parts = [matrix(j) * x[j : j + 1, :] for j in range(VARS)]
        return ((parts[0] + parts[1]) + (parts[2] + parts[3])) + (
            (parts[4] + parts[5]) + parts[6]
        )

    offsets = {}
    for k in range(TEAM):
        for r in range(ROWS):
            for h in range(PAIR):
                offsets[k, r, h] = product(
                    lambda j: column(k, h, r, j), rhs_in[k, r, h, 0:VARS, :]
                )

    def link_copy(way):
        return remote(
            link_out.at[way], link_in.at[way], link_sems, (way,), (s + (1 - 2 * way) * TEAM, g)
        )

    def arrive(way, there):
        @pl.when(there)
        def _():
            link_copy(way).wait_recv()

        return [jnp.where(there, link_in[way, h, 0:VARS, :], 0.0) for h in range(PAIR)]

    def depart(way, there, x):
        for h in range(PAIR):
            link_out[way, h, 0:VARS, :] = x[h]

        @pl.when(there)
        def _():
            link_copy(way).start()

    def upd_copy(k):
        q = lax.rem(place + k, TEAM)
        return remote(
            upd_out.at[q],
            upd_in.at[:, pl.ds(pl.multiple_of(place * PAIR * 8, PAIR * 8), PAIR * 8)],
            upd_sems,
            (k,),
            (base + q, g),
        )

    x = arrive(0, team > 0)
    stars = {}
    for k in range(TEAM):
        for r in range(ROWS):
            for h in range(PAIR):
                x[h] = offsets[k, r, h] + product(
                    lambda m: fmap[k, r, h, m, 0:VARS, :], x[h]
                )
                stars[k, r, h] = x[h]
    depart(0, team < n_teams - 1, x)
    x = arrive(1, team < n_teams - 1)
    for k in reversed(range(TEAM)):
        for r in reversed(range(ROWS)):
            for h in range(PAIR):
                x[h] = stars[k, r, h] + product(lambda m: bmap[k, r, h, m, 0:VARS, :], x[h])
                upd_out[k, r, h * 8 : h * 8 + VARS, :] = x[h]
    depart(1, team > 0, x)
    for k in far_first:
        upd_copy(k).start()
    own = pltpu.make_async_copy(
        upd_out.at[place],
        upd_in.at[:, pl.ds(pl.multiple_of(place * PAIR * 8, PAIR * 8), PAIR * 8)],
        local_sems.at[2],
    )
    own.start()
    own.wait()
    for k in range(1, TEAM):
        q = lax.rem(place + TEAM - k, TEAM)
        pltpu.make_async_remote_copy(
            src_ref=upd_out.at[place],
            dst_ref=upd_in.at[:, pl.ds(pl.multiple_of(q * PAIR * 8, PAIR * 8), PAIR * 8)],
            send_sem=upd_sems.at[0, k],
            recv_sem=upd_sems.at[1, k],
            device_id=(base + lax.rem(place + k, TEAM), g),
            device_id_type=MESH,
        ).wait_recv()
    for r in range(ROWS):
        for v in range(VARS):
            at = (r * VARS + v) * 8
            new_state[at : at + 8, :] = current[at : at + 8, :] + upd_in[r, pl.ds(v, 8, stride=8), :]

    keep[0].start()

    for k in range(1, TEAM):
        upd_copy(k).wait_send()
    for side in (0, 1):
        edge_copy(side).wait_send()
    for k in range(2, n_girth - 1):
        packet_copy(0, k).wait_send()
    for ds in (-1, 1):

        @pl.when(has(ds))
        def _():
            row_copy((ds + 1) // 2).wait_send()
            for k in range(1, n_girth):
                packet_copy(ds, k).wait_send()

    for way, there in ((0, team < n_teams - 1), (1, team > 0)):

        @pl.when(there)
        def _():
            link_copy(way).wait_send()

    for copy in keep:
        copy.wait()


def store(a, b, a_out, b_out, a_held, b_held, sems):
    steps = [
        pltpu.make_async_copy(*ends, sems.at[n])
        for n, ends in enumerate(((a, a_held), (b, b_held), (a_held, a_out), (b_held, b_out)))
    ]
    steps[0].start()
    steps[1].start()
    for n in range(2):
        steps[n].wait()
        steps[n + 2].start()
    for n in range(2):
        steps[n + 2].wait()


def per_device(
    state,
    propeller,
    donor_index,
    fringe_index,
    donor_weight,
    disk_mask,
    thrust,
    face,
    coupling,
    diag_inverse,
    lower_jacobian,
    upper_jacobian,
):
    n_stream, n_girth = lax.axis_size("stream"), lax.axis_size("girth")
    f32 = jnp.float32
    hbm = pl.BlockSpec(memory_space=pltpu.HBM)
    blocks = ROWS * VARS * 8
    padded = -(-ROWS * VARS * VARS // 8) * 8
    dma = pltpu.SemaphoreType.DMA
    given = (
        state.reshape(blocks, 128),
        propeller,
        donor_index,
        fringe_index,
        donor_weight,
        disk_mask.reshape(ROWS * 8, 128),
        thrust,
        face.reshape(ROWS * 6 * 8, 128),
        coupling,
        diag_inverse,
        lower_jacobian,
        upper_jacobian,
    )
    scalars = (6, 8, 10, 11)
    held = [
        (pltpu.SMEM if n in scalars else pltpu.VMEM)(x.shape, x.dtype) for n, x in enumerate(given)
    ]
    results = [jax.ShapeDtypeStruct((blocks, 128), f32)] * 2
    new_state, residual = pl.pallas_call(
        functools.partial(kernel, n_stream, n_girth),
        out_shape=results,
        in_specs=[hbm] * 12,
        out_specs=[hbm, hbm],
        scratch_shapes=held
        + [
            pltpu.VMEM((blocks, 128), f32),
            pltpu.VMEM((blocks, 128), f32),
            pltpu.VMEM((8, 128), f32),
            pltpu.VMEM((3, n_girth, 8, 128), f32),
            pltpu.VMEM((2, ROWS + 1, 8, 128), f32),
            pltpu.VMEM((2, ROWS + 1, 8, 128), f32),
            pltpu.VMEM((2, VARS * 8 + 8, 128), f32),
            pltpu.VMEM((2, VARS * 8 + 8, 128), f32),
            pltpu.VMEM((padded * 8, 128), f32),
            pltpu.VMEM((TEAM, PAIR, padded, 128), f32),
            pltpu.VMEM((TEAM, PAIR, padded, 128), f32),
            pltpu.VMEM((blocks, 128), f32),
            pltpu.VMEM((ROWS, VARS * 8, 128), f32),
            pltpu.VMEM((TEAM, ROWS, PAIR, 8, 128), f32),
            pltpu.VMEM((TEAM, ROWS, PAIR, 8, 128), f32),
            pltpu.VMEM((TEAM, ROWS, PAIR, VARS, 8, 128), f32),
            pltpu.VMEM((TEAM, ROWS, PAIR, VARS, 8, 128), f32),
            pltpu.VMEM((TEAM, ROWS, PAIR * 8, 128), f32),
            pltpu.VMEM((ROWS, TEAM * PAIR * 8, 128), f32),
            pltpu.VMEM((2, PAIR, 8, 128), f32),
            pltpu.VMEM((2, PAIR, 8, 128), f32),
            dma((2, 3, n_girth)),
            dma((2, 2)),
            dma((2, 2)),
            dma((2, TEAM)),
            dma((2, TEAM)),
            dma((2, TEAM)),
            dma((2, 2)),
            dma((3,)),
            dma((12,)),
            dma((2,)),
        ],
        compiler_params=pltpu.CompilerParams(
            collective_id=0, has_side_effects=True, vmem_limit_bytes=60 * 1024 * 1024
        ),
        cost_estimate=pl.CostEstimate(flops=12_000_000, bytes_accessed=500_000, transcendentals=0),
    )(*given)
    new_state, residual = pl.pallas_call(
        store,
        out_shape=results,
        in_specs=[hbm, hbm],
        out_specs=[hbm, hbm],
        scratch_shapes=[pltpu.VMEM((blocks, 128), f32)] * 2 + [dma((4,))],
        compiler_params=pltpu.CompilerParams(vmem_limit_bytes=60 * 1024 * 1024),
    )(new_state, residual)
    return new_state.reshape(state.shape), residual.reshape(state.shape)


def solution(mesh):
    placed = (
        P("stream", None, "girth", None),
        P(None, ("stream", "girth")),
        P(("stream", "girth"), None),
        P(("stream", "girth"), None),
        P(("stream", "girth"), None),
        P("stream", "girth", None),
        P(),
        P("stream", None, "girth", None),
        P(),
        P("stream", None, None, "girth", None),
        P(),
        P(),
    )
    return jax.shard_map(
        per_device,
        mesh=mesh,
        in_specs=placed,
        out_specs=(P("stream", None, "girth", None), P("stream", None, "girth", None)),
        check_vma=False,
    )
```

```python
import functools

import jax
import jax.numpy as jnp
from jax import lax
from jax.experimental import pallas as pl
from jax.experimental.pallas import tpu as pltpu
from jax.sharding import PartitionSpec as P

MESH = pl.DeviceIdType.MESH
PRECISE = lax.Precision.HIGHEST
VARS = 7
ROWS = 2
TEAM = 8
PAIR = 1
CAP = 8


def kernel(
    n_stream,
    n_girth,
    *refs,
):
    given, results, held = refs[:12], refs[12:14], refs[14:26]
    state, prop, donor, landing, weight, disk = held[:6]
    thrust, face, coupling, inverse, lower, upper = held[6:]
    (
        new_state,
        residual_out,
        packet,
        packets,
        edge_out,
        edge_in,
        row_out,
        row_in,
        planes,
        inv_out,
        inv_in,
        current,
        rhs_planes,
        rhs_out,
        rhs_in,
        fmap,
        bmap,
        upd_out,
        upd_in,
        link_out,
        link_in,
        packet_sems,
        edge_sems,
        row_sems,
        inv_sems,
        rhs_sems,
        upd_sems,
        link_sems,
        local_sems,
        load_sems,
        store_sems,
    ) = refs[26:]
    s, g = lax.axis_index("stream"), lax.axis_index("girth")
    base = (s // TEAM) * TEAM
    place = s - base
    team = s // TEAM
    n_teams = n_stream // TEAM
    slots = donor.shape[1]
    packs = n_girth if n_girth * slots <= 128 else 1

    def girth_at(k):
        return lax.rem(g + k + n_girth, n_girth)

    def remote(src, dst, sems, at, to):
        return pltpu.make_async_remote_copy(
            src_ref=src,
            dst_ref=dst,
            send_sem=sems.at[(0, *at)],
            recv_sem=sems.at[(1, *at)],
            device_id=to,
            device_id_type=MESH,
        )

    def has(ds):
        return jnp.logical_and(s + ds >= 0, s + ds < n_stream)

    def load(n):
        return pltpu.make_async_copy(given[n], held[n], load_sems.at[n])

    for n in (2, 3, 4, 1, 0, 9, 7, 8, 5, 6, 10, 11):
        load(n).start()

    barrier = pltpu.get_barrier_semaphore()

    def greet(to):
        pl.semaphore_signal(barrier, inc=1, device_id=to, device_id_type=MESH)

    for k in range(1, n_girth):
        greet((s, girth_at(k)))
    expected = n_girth - 1
    for ds in (-1, 1):

        @pl.when(has(ds))
        def _():
            for k in range(n_girth):
                greet((s + ds, girth_at(k)))

        expected = expected + jnp.where(has(ds), n_girth, 0)
    for k in range(1, TEAM):
        q = lax.rem(place + k, TEAM)
        far = jnp.logical_or(q - place > 1, place - q > 1)

        @pl.when(far)
        def _():
            greet((base + q, g))

        expected = expected + jnp.where(far, 1, 0)
    for ds in (-TEAM, TEAM):

        @pl.when(has(ds))
        def _():
            greet((s + ds, g))

        expected = expected + jnp.where(has(ds), 1, 0)

    for n in (1, 2, 3, 4):
        load(n).wait()

    lane = lax.broadcasted_iota(jnp.int32, (1, 128), 1)

    def spread(ref):
        return jnp.concatenate([ref[...]] * packs, axis=1) if packs > 1 else ref[...]

    donor_all = spread(donor)
    live = jnp.logical_and(lane // slots == lax.rem(g, packs), donor_all >= 0)
    cell = lax.broadcasted_iota(jnp.int32, (prop.shape[1], 128), 0)
    chosen = jnp.where(cell == jnp.where(live, donor_all, -1), 1.0, 0.0)
    taken = jnp.dot(prop[...], chosen, precision=PRECISE, preferred_element_type=jnp.float32)
    packet[0:VARS, :] = taken * jnp.where(live, spread(weight), 0.0)
    packet[VARS : VARS + 1, :] = jnp.where(live, spread(landing) + 1, 0).astype(jnp.float32)

    load(0).wait()
    for side, at in ((0, 0), (1, 7)):
        for r in range(ROWS):
            edge_out[side, r, 0:VARS, :] = state[pl.ds(r * VARS * 8 + at, VARS, stride=8), :]
            edge_out[side, r, VARS : VARS + 1, :] = jnp.zeros((1, 128), jnp.float32)
        edge_out[side, ROWS] = packet[...]
        row_out[side, 0 : VARS * 8, :] = state[
            side * (ROWS - 1) * VARS * 8 : (side * (ROWS - 1) + 1) * VARS * 8, :
        ]
        row_out[side, VARS * 8 :, :] = packet[...]

    load(9).wait()
    for r in range(ROWS):
        for i in range(VARS):
            for j in range(VARS):
                p = (r * VARS + i) * VARS + j
                planes[p * 8 : p * 8 + 8, :] = inverse[r, i, j].astype(jnp.float32)
    blocks = planes.shape[0] // 64
    planes[ROWS * VARS * VARS * 8 :, :] = jnp.zeros(
        (planes.shape[0] - ROWS * VARS * VARS * 8, 128), jnp.float32
    )
    for c in range(8):
        for b in range(blocks):
            inv_out[c // PAIR, c % PAIR, b * 8 : b * 8 + 8, :] = planes[
                pl.ds(b * 64 + c, 8, stride=8), :
            ]

    pl.semaphore_wait(barrier, expected)

    def packet_copy(ds, k):
        return remote(
            packet, packets.at[1 - ds, k], packet_sems, (1 - ds, k), (s + ds, girth_at(k))
        )

    def edge_copy(side):
        return remote(
            edge_out.at[side], edge_in.at[side], edge_sems, (side,), (s, girth_at(2 * side - 1))
        )

    def row_copy(side):
        return remote(
            row_out.at[side],
            row_in.at[side],
            row_sems,
            (side,),
            (s + 2 * side - 1, g),
        )

    for ds in (-1, 1):

        @pl.when(has(ds))
        def _():
            row_copy((ds + 1) // 2).start()
            for k in range(1, n_girth):
                packet_copy(ds, k).start()

    for side in (0, 1):
        edge_copy(side).start()
    for k in range(2, n_girth - 1):
        packet_copy(0, k).start()

    def team_copy(out, into, sems, k):
        q = lax.rem(place + k, TEAM)
        return remote(out.at[q], into.at[place], sems, (k,), (base + q, g))

    def team_arrival(out, into, sems, k):
        return pltpu.make_async_remote_copy(
            src_ref=out.at[place],
            dst_ref=into.at[lax.rem(place + TEAM - k, TEAM)],
            send_sem=sems.at[0, k],
            recv_sem=sems.at[1, k],
            device_id=(base + lax.rem(place + k, TEAM), g),
            device_id_type=MESH,
        )

    far_first = sorted(range(1, TEAM), key=lambda k: -min(k, TEAM - k))

    def own_copy(out, into, n):
        return pltpu.make_async_copy(out.at[place], into.at[place], local_sems.at[n])

    for k in far_first:
        team_copy(inv_out, inv_in, inv_sems, k).start()
    own_copy(inv_out, inv_in, 0).start()

    for side in (0, 1):
        edge_copy(side).wait_recv()
    for k in range(2, n_girth - 1):
        packet_copy(0, k).wait_recv()
    for ds in (-1, 1):

        @pl.when(has(ds))
        def _():
            row_copy((1 - ds) // 2).wait_recv()
            for k in range(1, n_girth):
                packet_copy(-ds, k).wait_recv()

    girth_cell = lax.broadcasted_iota(jnp.int32, (8, 128), 0)
    normal_cell = lax.broadcasted_iota(jnp.int32, (8, 128), 1)
    normal_rows = lax.broadcasted_iota(jnp.int32, (128, 128), 0)
    var_row = lax.broadcasted_iota(jnp.int32, (8, 128), 0)
    peer = lax.rem(lane, slots) // CAP

    def packet_from(o, k):
        if o != 1 and k == 0:
            return row_in[1 - o // 2, VARS * 8 :, :]
        if o == 1 and k in (1, n_girth - 1):
            return edge_in[1 if k == 1 else 0, ROWS]
        return packet[...] if k == 0 else packets[o, k]

    def landed(o, plan):
        total = None
        for first in range(0, n_girth, packs):
            tile = packet_from(o, first)
            for k in range(first + 1, first + packs):
                tile = tile + packet_from(o, k)
            code = tile[VARS : VARS + 1, :].astype(jnp.int32) - 1
            row, gc, nc = code >> 10, (code >> 7) & 7, code & 127
            nc = jnp.where(code >= 0, nc, -1)
            tile = jnp.where(var_row == VARS, 1.0, tile)
            part = lax.dot_general(
                jnp.concatenate(plan(tile, row, gc), axis=0),
                jnp.where(normal_rows == nc, 1.0, 0.0),
                (((1,), (1,)), ((), ())),
                precision=PRECISE,
                preferred_element_type=jnp.float32,
            )
            total = part if total is None else total + part
        return total

    def block_rows(r):
        def plan(tile, row, gc):
            here = jnp.logical_and(row == r, peer == g)
            hit = jnp.where(girth_cell == jnp.where(here, gc, -1), 1.0, 0.0)
            return [tile[v : v + 1, :] * hit for v in range(8)]

        return plan

    def own_plan(tile, row, gc):
        rows = block_rows(0)(tile, row, gc) + block_rows(1)(tile, row, gc)
        for at, side in ((7, -1), (0, 1)):
            for r in range(ROWS):
                here = (peer == girth_at(side)) & (row == r) & (gc == at)
                rows.append(tile * jnp.where(here, 1.0, 0.0))
        return rows

    def settle(found, raw):
        hit = found[VARS * 8 : VARS * 8 + 8] > 0.5
        return [jnp.where(hit, found[v * 8 : v * 8 + 8], raw(v)) for v in range(VARS)], hit

    own = landed(1, own_plan)
    cells, fringe = [], []
    for r in range(ROWS):
        found, hit = settle(
            own[r * 64 : r * 64 + 64], lambda v: state[(r * VARS + v) * 8 : (r * VARS + v) * 8 + 8, :]
        )
        cells.append(found)
        fringe.append(hit)
        for v in range(VARS):
            current[(r * VARS + v) * 8 : (r * VARS + v) * 8 + 8, :] = found[v]
    beside = {}
    for side in (0, 1):
        for r in range(ROWS):
            at = 128 + (side * ROWS + r) * 8
            found = own[at : at + 8]
            beside[side, r] = jnp.where(
                found[VARS : VARS + 1] > 0.5, found, edge_in[1 - side, r]
            )
    outer = []
    for o, r, side in ((0, 1, 1), (2, 0, 0)):
        found, _ = settle(
            landed(o, block_rows(r)), lambda v: row_in[side, v * 8 : v * 8 + 8, :]
        )
        outer.append([jnp.where(has(o - 1), x, 0.0) for x in found])

    for n in (5, 6, 7, 8, 10, 11):
        load(n).wait()
    for r in range(ROWS):
        here = cells[r]
        before = outer[0] if r == 0 else cells[r - 1]
        after = outer[1] if r == ROWS - 1 else cells[r + 1]
        in_disk = disk[r * 8 : r * 8 + 8, :].astype(jnp.float32)
        total = [in_disk * thrust[v] for v in range(VARS)]
        for d in range(6):
            step = []
            for v in range(VARS):
                x = here[v]
                if d == 0:
                    near = before[v]
                elif d == 1:
                    near = after[v]
                elif d == 2:
                    near = jnp.where(girth_cell == 0, beside[0, r][v : v + 1], pltpu.roll(x, 1, 0))
                elif d == 3:
                    near = jnp.where(girth_cell == 7, beside[1, r][v : v + 1], pltpu.roll(x, 7, 0))
                elif d == 4:
                    near = jnp.where(normal_cell == 0, 0.0, pltpu.roll(x, 1, 1))
                else:
                    near = jnp.where(normal_cell == 127, 0.0, pltpu.roll(x, 127, 1))
                step.append(near - x)
            area = face[(r * 6 + d) * 8 : (r * 6 + d) * 8 + 8, :]
            for i in range(VARS):
                flux = step[0] * coupling[d, i, 0]
                for j in range(1, VARS):
                    flux = flux + step[j] * coupling[d, i, j]
                total[i] = total[i] + area * flux
        for v in range(VARS):
            residual_out[(r * VARS + v) * 8 : (r * VARS + v) * 8 + 8, :] = total[v]
            rhs_planes[r, v * 8 : v * 8 + 8, :] = jnp.where(fringe[r], 0.0, -total[v])
        for c in range(8):
            rhs_out[c // PAIR, r, c % PAIR, 0:VARS, :] = rhs_planes[r, pl.ds(c, VARS, stride=8), :]

    for k in far_first:
        team_copy(rhs_out, rhs_in, rhs_sems, k).start()
    own_copy(rhs_out, rhs_in, 1).start()
    keep = [
        pltpu.make_async_copy(new_state, results[0], store_sems.at[0]),
        pltpu.make_async_copy(residual_out, results[1], store_sems.at[1]),
    ]
    keep[1].start()

    def column(k, h, r, j):
        return inv_in[k, h, pl.ds(r * VARS * VARS + j, VARS, stride=VARS), :]

    def matrices(k):
        for r in range(ROWS):
            for h in range(PAIR):
                cols = [column(k, h, r, j) for j in range(VARS)]
                for m in range(VARS):
                    f, b = cols[0] * lower[0, m], cols[0] * upper[0, m]
                    for j in range(1, VARS):
                        f = f + cols[j] * lower[j, m]
                        b = b + cols[j] * upper[j, m]
                    fmap[k, r, h, m, 0:VARS, :] = f
                    bmap[k, r, h, m, 0:VARS, :] = b

    def arrived(step):
        @pl.when(step == 0)
        def _():
            own_copy(inv_out, inv_in, 0).wait()

        for n, k in enumerate(reversed(far_first)):

            @pl.when(step == n + 1)
            def _():
                team_arrival(inv_out, inv_in, inv_sems, k).wait()

    def take_blocks(step, carry):
        arrived(step)
        away = (step + 1) // 2 * (2 * lax.rem(step + 1, 2) - 1)
        matrices(lax.rem(place - away + TEAM, TEAM))
        return carry

    lax.fori_loop(0, TEAM, take_blocks, 0)

    for k in range(1, TEAM):
        team_arrival(rhs_out, rhs_in, rhs_sems, k).wait()
    own_copy(rhs_out, rhs_in, 1).wait()

    def product(matrix, x):
        parts = [matrix(j) * x[j : j + 1, :] for j in range(VARS)]
        return ((parts[0] + parts[1]) + (parts[2] + parts[3])) + (
            (parts[4] + parts[5]) + parts[6]
        )

    offsets = {}
    for k in range(TEAM):
        for r in range(ROWS):
            for h in range(PAIR):
                offsets[k, r, h] = product(
                    lambda j: column(k, h, r, j), rhs_in[k, r, h, 0:VARS, :]
                )

    def link_copy(way):
        return remote(
            link_out.at[way], link_in.at[way], link_sems, (way,), (s + (1 - 2 * way) * TEAM, g)
        )

    def arrive(way, there):
        @pl.when(there)
        def _():
            link_copy(way).wait_recv()

        return [jnp.where(there, link_in[way, h, 0:VARS, :], 0.0) for h in range(PAIR)]

    def depart(way, there, x):
        for h in range(PAIR):
            link_out[way, h, 0:VARS, :] = x[h]

        @pl.when(there)
        def _():
            link_copy(way).start()

    def upd_copy(k):
        q = lax.rem(place + k, TEAM)
        return remote(
            upd_out.at[q],
            upd_in.at[:, pl.ds(pl.multiple_of(place * PAIR * 8, PAIR * 8), PAIR * 8)],
            upd_sems,
            (k,),
            (base + q, g),
        )

    x = arrive(0, team > 0)
    stars = {}
    for k in range(TEAM):
        for r in range(ROWS):
            for h in range(PAIR):
                x[h] = offsets[k, r, h] + product(
                    lambda m: fmap[k, r, h, m, 0:VARS, :], x[h]
                )
                stars[k, r, h] = x[h]
    depart(0, team < n_teams - 1, x)
    x = arrive(1, team < n_teams - 1)
    for k in reversed(range(TEAM)):
        for r in reversed(range(ROWS)):
            for h in range(PAIR):
                x[h] = stars[k, r, h] + product(lambda m: bmap[k, r, h, m, 0:VARS, :], x[h])
                upd_out[k, r, h * 8 : h * 8 + VARS, :] = x[h]
    depart(1, team > 0, x)
    for k in far_first:
        upd_copy(k).start()
    own = pltpu.make_async_copy(
        upd_out.at[place],
        upd_in.at[:, pl.ds(pl.multiple_of(place * PAIR * 8, PAIR * 8), PAIR * 8)],
        local_sems.at[2],
    )
    own.start()
    own.wait()
    for k in range(1, TEAM):
        q = lax.rem(place + TEAM - k, TEAM)
        pltpu.make_async_remote_copy(
            src_ref=upd_out.at[place],
            dst_ref=upd_in.at[:, pl.ds(pl.multiple_of(q * PAIR * 8, PAIR * 8), PAIR * 8)],
            send_sem=upd_sems.at[0, k],
            recv_sem=upd_sems.at[1, k],
            device_id=(base + lax.rem(place + k, TEAM), g),
            device_id_type=MESH,
        ).wait_recv()
    for r in range(ROWS):
        for v in range(VARS):
            at = (r * VARS + v) * 8
            new_state[at : at + 8, :] = current[at : at + 8, :] + upd_in[r, pl.ds(v, 8, stride=8), :]

    keep[0].start()

    for k in range(1, TEAM):
        upd_copy(k).wait_send()
    for side in (0, 1):
        edge_copy(side).wait_send()
    for k in range(2, n_girth - 1):
        packet_copy(0, k).wait_send()
    for ds in (-1, 1):

        @pl.when(has(ds))
        def _():
            row_copy((ds + 1) // 2).wait_send()
            for k in range(1, n_girth):
                packet_copy(ds, k).wait_send()

    for way, there in ((0, team < n_teams - 1), (1, team > 0)):

        @pl.when(there)
        def _():
            link_copy(way).wait_send()

    for copy in keep:
        copy.wait()


def per_device(
    state,
    propeller,
    donor_index,
    fringe_index,
    donor_weight,
    disk_mask,
    thrust,
    face,
    coupling,
    diag_inverse,
    lower_jacobian,
    upper_jacobian,
):
    n_stream, n_girth = lax.axis_size("stream"), lax.axis_size("girth")
    f32 = jnp.float32
    hbm = pl.BlockSpec(memory_space=pltpu.HBM)
    blocks = ROWS * VARS * 8
    padded = -(-ROWS * VARS * VARS // 8) * 8
    dma = pltpu.SemaphoreType.DMA
    given = (
        state.reshape(blocks, 128),
        propeller,
        donor_index,
        fringe_index,
        donor_weight,
        disk_mask.reshape(ROWS * 8, 128),
        thrust,
        face.reshape(ROWS * 6 * 8, 128),
        coupling,
        diag_inverse,
        lower_jacobian,
        upper_jacobian,
    )
    scalars = (6, 8, 10, 11)
    held = [
        (pltpu.SMEM if n in scalars else pltpu.VMEM)(x.shape, x.dtype) for n, x in enumerate(given)
    ]
    results = [jax.ShapeDtypeStruct((blocks, 128), f32)] * 2
    new_state, residual = pl.pallas_call(
        functools.partial(kernel, n_stream, n_girth),
        out_shape=results,
        in_specs=[hbm] * 12,
        out_specs=[hbm, hbm],
        scratch_shapes=held
        + [
            pltpu.VMEM((blocks, 128), f32),
            pltpu.VMEM((blocks, 128), f32),
            pltpu.VMEM((8, 128), f32),
            pltpu.VMEM((3, n_girth, 8, 128), f32),
            pltpu.VMEM((2, ROWS + 1, 8, 128), f32),
            pltpu.VMEM((2, ROWS + 1, 8, 128), f32),
            pltpu.VMEM((2, VARS * 8 + 8, 128), f32),
            pltpu.VMEM((2, VARS * 8 + 8, 128), f32),
            pltpu.VMEM((padded * 8, 128), f32),
            pltpu.VMEM((TEAM, PAIR, padded, 128), f32),
            pltpu.VMEM((TEAM, PAIR, padded, 128), f32),
            pltpu.VMEM((blocks, 128), f32),
            pltpu.VMEM((ROWS, VARS * 8, 128), f32),
            pltpu.VMEM((TEAM, ROWS, PAIR, 8, 128), f32),
            pltpu.VMEM((TEAM, ROWS, PAIR, 8, 128), f32),
            pltpu.VMEM((TEAM, ROWS, PAIR, VARS, 8, 128), f32),
            pltpu.VMEM((TEAM, ROWS, PAIR, VARS, 8, 128), f32),
            pltpu.VMEM((TEAM, ROWS, PAIR * 8, 128), f32),
            pltpu.VMEM((ROWS, TEAM * PAIR * 8, 128), f32),
            pltpu.VMEM((2, PAIR, 8, 128), f32),
            pltpu.VMEM((2, PAIR, 8, 128), f32),
            dma((2, 3, n_girth)),
            dma((2, 2)),
            dma((2, 2)),
            dma((2, TEAM)),
            dma((2, TEAM)),
            dma((2, TEAM)),
            dma((2, 2)),
            dma((3,)),
            dma((12,)),
            dma((2,)),
        ],
        compiler_params=pltpu.CompilerParams(
            collective_id=0, has_side_effects=True, vmem_limit_bytes=60 * 1024 * 1024
        ),
        cost_estimate=pl.CostEstimate(flops=12_000_000, bytes_accessed=500_000, transcendentals=0),
    )(*given)
    return new_state.reshape(state.shape), residual.reshape(state.shape)


def solution(mesh):
    placed = (
        P("stream", None, "girth", None),
        P(None, ("stream", "girth")),
        P(("stream", "girth"), None),
        P(("stream", "girth"), None),
        P(("stream", "girth"), None),
        P("stream", "girth", None),
        P(),
        P("stream", None, "girth", None),
        P(),
        P("stream", None, None, "girth", None),
        P(),
        P(),
    )
    return jax.shard_map(
        per_device,
        mesh=mesh,
        in_specs=placed,
        out_specs=(P("stream", None, "girth", None), P("stream", None, "girth", None)),
        check_vma=False,
    )
```

```python
import functools

import jax
import jax.numpy as jnp
from jax import lax
from jax.experimental import pallas as pl
from jax.experimental.pallas import tpu as pltpu
from jax.sharding import PartitionSpec as P

MESH = pl.DeviceIdType.MESH
PRECISE = lax.Precision.HIGHEST
VARS = 7
ROWS = 2
TEAM = 4
PAIR = 2
CAP = 8


def kernel(
    n_stream,
    n_girth,
    *refs,
):
    given, results, held = refs[:12], refs[12:14], refs[14:26]
    state, prop, donor, landing, weight, disk = held[:6]
    thrust, face, coupling, inverse, lower, upper = held[6:]
    (
        new_state,
        residual_out,
        packet,
        packets,
        edge_out,
        edge_in,
        row_out,
        row_in,
        planes,
        inv_out,
        inv_in,
        current,
        rhs_planes,
        rhs_out,
        rhs_in,
        fmap,
        bmap,
        reply,
        answer,
        upd_out,
        upd_in,
        link_out,
        link_in,
        packet_sems,
        edge_sems,
        row_sems,
        inv_sems,
        rhs_sems,
        upd_sems,
        link_sems,
        local_sems,
        load_sems,
        store_sems,
    ) = refs[26:]
    s, g = lax.axis_index("stream"), lax.axis_index("girth")
    base = (s // TEAM) * TEAM
    place = s - base
    team = s // TEAM
    n_teams = n_stream // TEAM
    slots = donor.shape[1]
    packs = n_girth if n_girth * slots <= 128 else 1

    def girth_at(k):
        return lax.rem(g + k + n_girth, n_girth)

    def remote(src, dst, sems, at, to):
        return pltpu.make_async_remote_copy(
            src_ref=src,
            dst_ref=dst,
            send_sem=sems.at[(0, *at)],
            recv_sem=sems.at[(1, *at)],
            device_id=to,
            device_id_type=MESH,
        )

    def has(ds):
        return jnp.logical_and(s + ds >= 0, s + ds < n_stream)

    def load(n):
        return pltpu.make_async_copy(given[n], held[n], load_sems.at[n])

    for n in (2, 3, 4, 1, 0, 9, 7, 8, 5, 6, 10, 11):
        load(n).start()

    barrier = pltpu.get_barrier_semaphore()

    def greet(to):
        pl.semaphore_signal(barrier, inc=1, device_id=to, device_id_type=MESH)

    for k in range(1, n_girth):
        greet((s, girth_at(k)))
    expected = n_girth - 1
    for ds in (-1, 1):

        @pl.when(has(ds))
        def _():
            for k in range(n_girth):
                greet((s + ds, girth_at(k)))

        expected = expected + jnp.where(has(ds), n_girth, 0)
    for k in range(1, TEAM):
        q = lax.rem(place + k, TEAM)
        far = jnp.logical_or(q - place > 1, place - q > 1)

        @pl.when(far)
        def _():
            greet((base + q, g))

        expected = expected + jnp.where(far, 1, 0)
    for ds in (-TEAM, TEAM):

        @pl.when(has(ds))
        def _():
            greet((s + ds, g))

        expected = expected + jnp.where(has(ds), 1, 0)

    for n in (1, 2, 3, 4):
        load(n).wait()

    lane = lax.broadcasted_iota(jnp.int32, (1, 128), 1)

    def spread(ref):
        return jnp.concatenate([ref[...]] * packs, axis=1) if packs > 1 else ref[...]

    donor_all = spread(donor)
    live = jnp.logical_and(lane // slots == lax.rem(g, packs), donor_all >= 0)
    cell = lax.broadcasted_iota(jnp.int32, (prop.shape[1], 128), 0)
    chosen = jnp.where(cell == jnp.where(live, donor_all, -1), 1.0, 0.0)
    taken = jnp.dot(prop[...], chosen, precision=PRECISE, preferred_element_type=jnp.float32)
    packet[0:VARS, :] = taken * jnp.where(live, spread(weight), 0.0)
    packet[VARS : VARS + 1, :] = jnp.where(live, spread(landing) + 1, 0).astype(jnp.float32)

    load(0).wait()
    for side, at in ((0, 0), (1, 7)):
        for r in range(ROWS):
            edge_out[side, r, 0:VARS, :] = state[pl.ds(r * VARS * 8 + at, VARS, stride=8), :]
            edge_out[side, r, VARS : VARS + 1, :] = jnp.zeros((1, 128), jnp.float32)
        edge_out[side, ROWS] = packet[...]
        row_out[side, 0 : VARS * 8, :] = state[
            side * (ROWS - 1) * VARS * 8 : (side * (ROWS - 1) + 1) * VARS * 8, :
        ]
        row_out[side, VARS * 8 :, :] = packet[...]

    load(9).wait()
    for r in range(ROWS):
        for i in range(VARS):
            for j in range(VARS):
                p = (r * VARS + i) * VARS + j
                planes[p * 8 : p * 8 + 8, :] = inverse[r, i, j].astype(jnp.float32)
    blocks = planes.shape[0] // 64
    planes[ROWS * VARS * VARS * 8 :, :] = jnp.zeros(
        (planes.shape[0] - ROWS * VARS * VARS * 8, 128), jnp.float32
    )
    for c in range(8):
        for b in range(blocks):
            inv_out[c // PAIR, c % PAIR, b * 8 : b * 8 + 8, :] = planes[
                pl.ds(b * 64 + c, 8, stride=8), :
            ]

    pl.semaphore_wait(barrier, expected)

    def packet_copy(ds, k):
        return remote(
            packet, packets.at[1 - ds, k], packet_sems, (1 - ds, k), (s + ds, girth_at(k))
        )

    def edge_copy(side):
        return remote(
            edge_out.at[side], edge_in.at[side], edge_sems, (side,), (s, girth_at(2 * side - 1))
        )

    def row_copy(side):
        return remote(
            row_out.at[side],
            row_in.at[side],
            row_sems,
            (side,),
            (s + 2 * side - 1, g),
        )

    for ds in (-1, 1):

        @pl.when(has(ds))
        def _():
            row_copy((ds + 1) // 2).start()
            for k in range(1, n_girth):
                packet_copy(ds, k).start()

    for side in (0, 1):
        edge_copy(side).start()
    for k in range(2, n_girth - 1):
        packet_copy(0, k).start()

    def team_copy(out, into, sems, k):
        q = lax.rem(place + k, TEAM)
        return remote(out.at[q], into.at[place], sems, (k,), (base + q, g))

    def team_arrival(out, into, sems, k):
        return pltpu.make_async_remote_copy(
            src_ref=out.at[place],
            dst_ref=into.at[lax.rem(place + TEAM - k, TEAM)],
            send_sem=sems.at[0, k],
            recv_sem=sems.at[1, k],
            device_id=(base + lax.rem(place + k, TEAM), g),
            device_id_type=MESH,
        )

    far_first = sorted(range(1, TEAM), key=lambda k: -min(k, TEAM - k))

    def own_copy(out, into, n):
        return pltpu.make_async_copy(out.at[place], into.at[place], local_sems.at[n])

    for k in far_first:
        team_copy(inv_out, inv_in, inv_sems, k).start()
    own_copy(inv_out, inv_in, 0).start()

    for side in (0, 1):
        edge_copy(side).wait_recv()
    for k in range(2, n_girth - 1):
        packet_copy(0, k).wait_recv()
    for ds in (-1, 1):

        @pl.when(has(ds))
        def _():
            row_copy((1 - ds) // 2).wait_recv()
            for k in range(1, n_girth):
                packet_copy(-ds, k).wait_recv()

    girth_cell = lax.broadcasted_iota(jnp.int32, (8, 128), 0)
    normal_cell = lax.broadcasted_iota(jnp.int32, (8, 128), 1)
    normal_rows = lax.broadcasted_iota(jnp.int32, (128, 128), 0)
    var_row = lax.broadcasted_iota(jnp.int32, (8, 128), 0)
    peer = lax.rem(lane, slots) // CAP

    def packet_from(o, k):
        if o != 1 and k == 0:
            return row_in[1 - o // 2, VARS * 8 :, :]
        if o == 1 and k in (1, n_girth - 1):
            return edge_in[1 if k == 1 else 0, ROWS]
        return packet[...] if k == 0 else packets[o, k]

    def landed(o, plan):
        total = None
        for first in range(0, n_girth, packs):
            tile = packet_from(o, first)
            for k in range(first + 1, first + packs):
                tile = tile + packet_from(o, k)
            code = tile[VARS : VARS + 1, :].astype(jnp.int32) - 1
            row, gc, nc = code >> 10, (code >> 7) & 7, code & 127
            nc = jnp.where(code >= 0, nc, -1)
            tile = jnp.where(var_row == VARS, 1.0, tile)
            part = lax.dot_general(
                jnp.concatenate(plan(tile, row, gc), axis=0),
                jnp.where(normal_rows == nc, 1.0, 0.0),
                (((1,), (1,)), ((), ())),
                precision=PRECISE,
                preferred_element_type=jnp.float32,
            )
            total = part if total is None else total + part
        return total

    def block_rows(r):
        def plan(tile, row, gc):
            here = jnp.logical_and(row == r, peer == g)
            hit = jnp.where(girth_cell == jnp.where(here, gc, -1), 1.0, 0.0)
            return [tile[v : v + 1, :] * hit for v in range(8)]

        return plan

    def own_plan(tile, row, gc):
        rows = block_rows(0)(tile, row, gc) + block_rows(1)(tile, row, gc)
        for at, side in ((7, -1), (0, 1)):
            for r in range(ROWS):
                here = (peer == girth_at(side)) & (row == r) & (gc == at)
                rows.append(tile * jnp.where(here, 1.0, 0.0))
        return rows

    def settle(found, raw):
        hit = found[VARS * 8 : VARS * 8 + 8] > 0.5
        return [jnp.where(hit, found[v * 8 : v * 8 + 8], raw(v)) for v in range(VARS)], hit

    own = landed(1, own_plan)
    cells, fringe = [], []
    for r in range(ROWS):
        found, hit = settle(
            own[r * 64 : r * 64 + 64], lambda v: state[(r * VARS + v) * 8 : (r * VARS + v) * 8 + 8, :]
        )
        cells.append(found)
        fringe.append(hit)
        for v in range(VARS):
            current[(r * VARS + v) * 8 : (r * VARS + v) * 8 + 8, :] = found[v]
    beside = {}
    for side in (0, 1):
        for r in range(ROWS):
            at = 128 + (side * ROWS + r) * 8
            found = own[at : at + 8]
            beside[side, r] = jnp.where(
                found[VARS : VARS + 1] > 0.5, found, edge_in[1 - side, r]
            )
    outer = []
    for o, r, side in ((0, 1, 1), (2, 0, 0)):
        found, _ = settle(
            landed(o, block_rows(r)), lambda v: row_in[side, v * 8 : v * 8 + 8, :]
        )
        outer.append([jnp.where(has(o - 1), x, 0.0) for x in found])

    for n in (5, 6, 7, 8, 10, 11):
        load(n).wait()
    for r in range(ROWS):
        here = cells[r]
        before = outer[0] if r == 0 else cells[r - 1]
        after = outer[1] if r == ROWS - 1 else cells[r + 1]
        in_disk = disk[r * 8 : r * 8 + 8, :].astype(jnp.float32)
        total = [in_disk * thrust[v] for v in range(VARS)]
        for d in range(6):
            step = []
            for v in range(VARS):
                x = here[v]
                if d == 0:
                    near = before[v]
                elif d == 1:
                    near = after[v]
                elif d == 2:
                    near = jnp.where(girth_cell == 0, beside[0, r][v : v + 1], pltpu.roll(x, 1, 0))
                elif d == 3:
                    near = jnp.where(girth_cell == 7, beside[1, r][v : v + 1], pltpu.roll(x, 7, 0))
                elif d == 4:
                    near = jnp.where(normal_cell == 0, 0.0, pltpu.roll(x, 1, 1))
                else:
                    near = jnp.where(normal_cell == 127, 0.0, pltpu.roll(x, 127, 1))
                step.append(near - x)
            area = face[(r * 6 + d) * 8 : (r * 6 + d) * 8 + 8, :]
            for i in range(VARS):
                flux = step[0] * coupling[d, i, 0]
                for j in range(1, VARS):
                    flux = flux + step[j] * coupling[d, i, j]
                total[i] = total[i] + area * flux
        for v in range(VARS):
            residual_out[(r * VARS + v) * 8 : (r * VARS + v) * 8 + 8, :] = total[v]
            rhs_planes[r, v * 8 : v * 8 + 8, :] = jnp.where(fringe[r], 0.0, -total[v])
        for c in range(8):
            rhs_out[c // PAIR, r, c % PAIR, 0:VARS, :] = rhs_planes[r, pl.ds(c, VARS, stride=8), :]

    for k in far_first:
        team_copy(rhs_out, rhs_in, rhs_sems, k).start()
    own_copy(rhs_out, rhs_in, 1).start()
    keep = [
        pltpu.make_async_copy(new_state, results[0], store_sems.at[0]),
        pltpu.make_async_copy(residual_out, results[1], store_sems.at[1]),
    ]
    keep[1].start()

    def column(k, h, r, j):
        return inv_in[k, h, pl.ds(r * VARS * VARS + j, VARS, stride=VARS), :]

    def matrices(k):
        for r in range(ROWS):
            for h in range(PAIR):
                cols = [column(k, h, r, j) for j in range(VARS)]
                for m in range(VARS):
                    f, b = cols[0] * lower[0, m], cols[0] * upper[0, m]
                    for j in range(1, VARS):
                        f = f + cols[j] * lower[j, m]
                        b = b + cols[j] * upper[j, m]
                    fmap[k, r, h, m, 0:VARS, :] = f
                    bmap[k, r, h, m, 0:VARS, :] = b

    def arrived(step):
        @pl.when(step == 0)
        def _():
            own_copy(inv_out, inv_in, 0).wait()

        for n, k in enumerate(reversed(far_first)):

            @pl.when(step == n + 1)
            def _():
                team_arrival(inv_out, inv_in, inv_sems, k).wait()

    def take_blocks(step, carry):
        arrived(step)
        away = (step + 1) // 2 * (2 * lax.rem(step + 1, 2) - 1)
        matrices(lax.rem(place - away + TEAM, TEAM))
        return carry

    lax.fori_loop(0, TEAM, take_blocks, 0)

    for k in range(1, TEAM):
        team_arrival(rhs_out, rhs_in, rhs_sems, k).wait()
    own_copy(rhs_out, rhs_in, 1).wait()

    def product(matrix, x):
        parts = [matrix(j) * x[j : j + 1, :] for j in range(VARS)]
        return ((parts[0] + parts[1]) + (parts[2] + parts[3])) + (
            (parts[4] + parts[5]) + parts[6]
        )

    offsets = {}
    for k in range(TEAM):
        for r in range(ROWS):
            for h in range(PAIR):
                offsets[k, r, h] = product(
                    lambda j: column(k, h, r, j), rhs_in[k, r, h, 0:VARS, :]
                )

    def link_copy(way):
        return remote(
            link_out.at[way], link_in.at[way], link_sems, (way,), (s + (1 - 2 * way) * TEAM, g)
        )

    def arrive(way, there):
        @pl.when(there)
        def _():
            link_copy(way).wait_recv()

        return [jnp.where(there, link_in[way, h, 0:VARS, :], 0.0) for h in range(PAIR)]

    def depart(way, there, x):
        for h in range(PAIR):
            link_out[way, h, 0:VARS, :] = x[h]

        @pl.when(there)
        def _():
            link_copy(way).start()

    def upd_copy(k):
        q = lax.rem(place + k, TEAM)
        return remote(
            upd_out.at[q],
            upd_in.at[:, pl.ds(pl.multiple_of(place * PAIR * 8, PAIR * 8), PAIR * 8)],
            upd_sems,
            (k,),
            (base + q, g),
        )

    last = team == n_teams - 1
    steps = TEAM * ROWS
    row_of = lax.broadcasted_iota(jnp.int32, (VARS, 128), 0)
    unit = tuple(jnp.where(row_of == n, 1.0, 0.0) for _ in range(PAIR) for n in range(VARS))

    def factor(maps, t, h):
        return lambda m: maps[t // ROWS, lax.rem(t, ROWS), h, m, 0:VARS, :]

    def forward(x):
        stars = []
        for t in range(steps):
            k, r = divmod(t, ROWS)
            x = [offsets[k, r, h] + product(factor(fmap, t, h), x[h]) for h in range(PAIR)]
            stars.append(x)
        return stars

    def backward(stars):
        x, updates = stars[-1], [stars[-1]]
        for t in reversed(range(steps - 1)):
            x = [stars[t][h] + product(factor(bmap, t, h), x[h]) for h in range(PAIR)]
            updates.append(x)
        return updates[::-1]

    def respond(maps, into, start, reverse, plus=None):
        def advance(n, columns):
            t = steps - 1 - n if reverse else n
            out = []
            for h in range(PAIR):
                for v in range(VARS):
                    x = product(factor(maps, t, h), columns[h * VARS + v])
                    if plus is not None:
                        x = x + factor(plus, t, h)(v)
                    into[t // ROWS, lax.rem(t, ROWS), h, v, 0:VARS, :] = x
                    out.append(x)
            return tuple(out)

        lax.fori_loop(0, steps, advance, start)

    def finish(updates, entering):
        first = None
        for t in range(steps):
            k, r = divmod(t, ROWS)
            x = [
                updates[t][h] + product(factor(answer, t, h), entering[h]) for h in range(PAIR)
            ]
            for h in range(PAIR):
                upd_out[k, r, h * 8 : h * 8 + VARS, :] = x[h]
            if t == 0:
                depart(1, team > 0, x)

    nothing = [jnp.zeros((VARS, 128), jnp.float32)] * PAIR

    @pl.when(last)
    def _():
        updates = backward(forward(nothing))
        respond(fmap, reply, unit, False)
        respond(bmap, answer, tuple(jnp.zeros_like(x) for x in unit), True, reply)
        finish(updates, arrive(0, team > 0))

    @pl.when(jnp.logical_not(last))
    def _():
        stars = forward(arrive(0, team > 0))
        depart(0, team < n_teams - 1, stars[-1])
        updates = backward(stars)
        respond(bmap, answer, unit, True)
        finish(updates, arrive(1, team < n_teams - 1))

    for k in far_first:
        upd_copy(k).start()
    own = pltpu.make_async_copy(
        upd_out.at[place],
        upd_in.at[:, pl.ds(pl.multiple_of(place * PAIR * 8, PAIR * 8), PAIR * 8)],
        local_sems.at[2],
    )
    own.start()
    own.wait()
    for k in range(1, TEAM):
        q = lax.rem(place + TEAM - k, TEAM)
        pltpu.make_async_remote_copy(
            src_ref=upd_out.at[place],
            dst_ref=upd_in.at[:, pl.ds(pl.multiple_of(q * PAIR * 8, PAIR * 8), PAIR * 8)],
            send_sem=upd_sems.at[0, k],
            recv_sem=upd_sems.at[1, k],
            device_id=(base + lax.rem(place + k, TEAM), g),
            device_id_type=MESH,
        ).wait_recv()
    for r in range(ROWS):
        for v in range(VARS):
            at = (r * VARS + v) * 8
            new_state[at : at + 8, :] = current[at : at + 8, :] + upd_in[r, pl.ds(v, 8, stride=8), :]

    keep[0].start()

    for k in range(1, TEAM):
        upd_copy(k).wait_send()
    for side in (0, 1):
        edge_copy(side).wait_send()
    for k in range(2, n_girth - 1):
        packet_copy(0, k).wait_send()
    for ds in (-1, 1):

        @pl.when(has(ds))
        def _():
            row_copy((ds + 1) // 2).wait_send()
            for k in range(1, n_girth):
                packet_copy(ds, k).wait_send()

    for way, there in ((0, team < n_teams - 1), (1, team > 0)):

        @pl.when(there)
        def _():
            link_copy(way).wait_send()

    for copy in keep:
        copy.wait()


def store(a, b, a_out, b_out, a_held, b_held, sems):
    steps = [
        pltpu.make_async_copy(*ends, sems.at[n])
        for n, ends in enumerate(((a, a_held), (b, b_held), (a_held, a_out), (b_held, b_out)))
    ]
    steps[0].start()
    steps[1].start()
    for n in range(2):
        steps[n].wait()
        steps[n + 2].start()
    for n in range(2):
        steps[n + 2].wait()


def per_device(
    state,
    propeller,
    donor_index,
    fringe_index,
    donor_weight,
    disk_mask,
    thrust,
    face,
    coupling,
    diag_inverse,
    lower_jacobian,
    upper_jacobian,
):
    n_stream, n_girth = lax.axis_size("stream"), lax.axis_size("girth")
    f32 = jnp.float32
    hbm = pl.BlockSpec(memory_space=pltpu.HBM)
    blocks = ROWS * VARS * 8
    padded = -(-ROWS * VARS * VARS // 8) * 8
    dma = pltpu.SemaphoreType.DMA
    given = (
        state.reshape(blocks, 128),
        propeller,
        donor_index,
        fringe_index,
        donor_weight,
        disk_mask.reshape(ROWS * 8, 128),
        thrust,
        face.reshape(ROWS * 6 * 8, 128),
        coupling,
        diag_inverse,
        lower_jacobian,
        upper_jacobian,
    )
    scalars = (6, 8, 10, 11)
    held = [
        (pltpu.SMEM if n in scalars else pltpu.VMEM)(x.shape, x.dtype) for n, x in enumerate(given)
    ]
    results = [jax.ShapeDtypeStruct((blocks, 128), f32)] * 2
    new_state, residual = pl.pallas_call(
        functools.partial(kernel, n_stream, n_girth),
        out_shape=results,
        in_specs=[hbm] * 12,
        out_specs=[hbm, hbm],
        scratch_shapes=held
        + [
            pltpu.VMEM((blocks, 128), f32),
            pltpu.VMEM((blocks, 128), f32),
            pltpu.VMEM((8, 128), f32),
            pltpu.VMEM((3, n_girth, 8, 128), f32),
            pltpu.VMEM((2, ROWS + 1, 8, 128), f32),
            pltpu.VMEM((2, ROWS + 1, 8, 128), f32),
            pltpu.VMEM((2, VARS * 8 + 8, 128), f32),
            pltpu.VMEM((2, VARS * 8 + 8, 128), f32),
            pltpu.VMEM((padded * 8, 128), f32),
            pltpu.VMEM((TEAM, PAIR, padded, 128), f32),
            pltpu.VMEM((TEAM, PAIR, padded, 128), f32),
            pltpu.VMEM((blocks, 128), f32),
            pltpu.VMEM((ROWS, VARS * 8, 128), f32),
            pltpu.VMEM((TEAM, ROWS, PAIR, 8, 128), f32),
            pltpu.VMEM((TEAM, ROWS, PAIR, 8, 128), f32),
            pltpu.VMEM((TEAM, ROWS, PAIR, VARS, 8, 128), f32),
            pltpu.VMEM((TEAM, ROWS, PAIR, VARS, 8, 128), f32),
            pltpu.VMEM((TEAM, ROWS, PAIR, VARS, 8, 128), f32),
            pltpu.VMEM((TEAM, ROWS, PAIR, VARS, 8, 128), f32),
            pltpu.VMEM((TEAM, ROWS, PAIR * 8, 128), f32),
            pltpu.VMEM((ROWS, TEAM * PAIR * 8, 128), f32),
            pltpu.VMEM((2, PAIR, 8, 128), f32),
            pltpu.VMEM((2, PAIR, 8, 128), f32),
            dma((2, 3, n_girth)),
            dma((2, 2)),
            dma((2, 2)),
            dma((2, TEAM)),
            dma((2, TEAM)),
            dma((2, TEAM)),
            dma((2, 2)),
            dma((3,)),
            dma((12,)),
            dma((2,)),
        ],
        compiler_params=pltpu.CompilerParams(
            collective_id=0, has_side_effects=True, vmem_limit_bytes=60 * 1024 * 1024
        ),
        cost_estimate=pl.CostEstimate(flops=12_000_000, bytes_accessed=500_000, transcendentals=0),
    )(*given)
    new_state, residual = pl.pallas_call(
        store,
        out_shape=results,
        in_specs=[hbm, hbm],
        out_specs=[hbm, hbm],
        scratch_shapes=[pltpu.VMEM((blocks, 128), f32)] * 2 + [dma((4,))],
        compiler_params=pltpu.CompilerParams(vmem_limit_bytes=60 * 1024 * 1024),
    )(new_state, residual)
    return new_state.reshape(state.shape), residual.reshape(state.shape)


def solution(mesh):
    placed = (
        P("stream", None, "girth", None),
        P(None, ("stream", "girth")),
        P(("stream", "girth"), None),
        P(("stream", "girth"), None),
        P(("stream", "girth"), None),
        P("stream", "girth", None),
        P(),
        P("stream", None, "girth", None),
        P(),
        P("stream", None, None, "girth", None),
        P(),
        P(),
    )
    return jax.shard_map(
        per_device,
        mesh=mesh,
        in_specs=placed,
        out_specs=(P("stream", None, "girth", None), P("stream", None, "girth", None)),
        check_vma=False,
    )
```

```python
import functools

import jax
import jax.numpy as jnp
from jax import lax
from jax.experimental import pallas as pl
from jax.experimental.pallas import tpu as pltpu
from jax.sharding import PartitionSpec as P

MESH = pl.DeviceIdType.MESH
PRECISE = lax.Precision.HIGHEST
VARS = 7
ROWS = 2
TEAM = 4
PAIR = 2
CAP = 8


def kernel(
    n_stream,
    n_girth,
    *refs,
):
    given, results, held = refs[:12], refs[12:14], refs[14:26]
    state, prop, donor, landing, weight, disk = held[:6]
    thrust, face, coupling, inverse, lower, upper = held[6:]
    (
        new_state,
        residual_out,
        packet,
        packets,
        edge_out,
        edge_in,
        row_out,
        row_in,
        planes,
        inv_out,
        inv_in,
        current,
        rhs_planes,
        rhs_out,
        rhs_in,
        fmap,
        bmap,
        upd_out,
        upd_in,
        link_out,
        link_in,
        packet_sems,
        edge_sems,
        row_sems,
        inv_sems,
        rhs_sems,
        upd_sems,
        link_sems,
        local_sems,
        load_sems,
        store_sems,
    ) = refs[26:]
    s, g = lax.axis_index("stream"), lax.axis_index("girth")
    base = (s // TEAM) * TEAM
    place = s - base
    team = s // TEAM
    n_teams = n_stream // TEAM
    slots = donor.shape[1]
    packs = n_girth if n_girth * slots <= 128 else 1

    def girth_at(k):
        return lax.rem(g + k + n_girth, n_girth)

    def remote(src, dst, sems, at, to):
        return pltpu.make_async_remote_copy(
            src_ref=src,
            dst_ref=dst,
            send_sem=sems.at[(0, *at)],
            recv_sem=sems.at[(1, *at)],
            device_id=to,
            device_id_type=MESH,
        )

    def has(ds):
        return jnp.logical_and(s + ds >= 0, s + ds < n_stream)

    def load(n):
        return pltpu.make_async_copy(given[n], held[n], load_sems.at[n])

    for n in (2, 3, 4, 1, 0, 9, 7, 8, 5, 6, 10, 11):
        load(n).start()

    barrier = pltpu.get_barrier_semaphore()

    def greet(to):
        pl.semaphore_signal(barrier, inc=1, device_id=to, device_id_type=MESH)

    for k in range(1, n_girth):
        greet((s, girth_at(k)))
    expected = n_girth - 1
    for ds in (-1, 1):

        @pl.when(has(ds))
        def _():
            for k in range(n_girth):
                greet((s + ds, girth_at(k)))

        expected = expected + jnp.where(has(ds), n_girth, 0)
    for k in range(1, TEAM):
        q = lax.rem(place + k, TEAM)
        far = jnp.logical_or(q - place > 1, place - q > 1)

        @pl.when(far)
        def _():
            greet((base + q, g))

        expected = expected + jnp.where(far, 1, 0)
    for ds in (-TEAM, TEAM):

        @pl.when(has(ds))
        def _():
            greet((s + ds, g))

        expected = expected + jnp.where(has(ds), 1, 0)

    for n in (1, 2, 3, 4):
        load(n).wait()

    lane = lax.broadcasted_iota(jnp.int32, (1, 128), 1)

    def spread(ref):
        return jnp.concatenate([ref[...]] * packs, axis=1) if packs > 1 else ref[...]

    donor_all = spread(donor)
    live = jnp.logical_and(lane // slots == lax.rem(g, packs), donor_all >= 0)
    cell = lax.broadcasted_iota(jnp.int32, (prop.shape[1], 128), 0)
    chosen = jnp.where(cell == jnp.where(live, donor_all, -1), 1.0, 0.0)
    taken = jnp.dot(prop[...], chosen, precision=PRECISE, preferred_element_type=jnp.float32)
    packet[0:VARS, :] = taken * jnp.where(live, spread(weight), 0.0)
    packet[VARS : VARS + 1, :] = jnp.where(live, spread(landing) + 1, 0).astype(jnp.float32)

    load(0).wait()
    for side, at in ((0, 0), (1, 7)):
        for r in range(ROWS):
            edge_out[side, r, 0:VARS, :] = state[pl.ds(r * VARS * 8 + at, VARS, stride=8), :]
            edge_out[side, r, VARS : VARS + 1, :] = jnp.zeros((1, 128), jnp.float32)
        edge_out[side, ROWS] = packet[...]
        row_out[side, 0 : VARS * 8, :] = state[
            side * (ROWS - 1) * VARS * 8 : (side * (ROWS - 1) + 1) * VARS * 8, :
        ]
        row_out[side, VARS * 8 :, :] = packet[...]

    load(9).wait()
    for r in range(ROWS):
        for i in range(VARS):
            for j in range(VARS):
                p = (r * VARS + i) * VARS + j
                planes[p * 8 : p * 8 + 8, :] = inverse[r, i, j].astype(jnp.float32)
    blocks = planes.shape[0] // 64
    planes[ROWS * VARS * VARS * 8 :, :] = jnp.zeros(
        (planes.shape[0] - ROWS * VARS * VARS * 8, 128), jnp.float32
    )
    for c in range(8):
        for b in range(blocks):
            inv_out[c // PAIR, c % PAIR, b * 8 : b * 8 + 8, :] = planes[
                pl.ds(b * 64 + c, 8, stride=8), :
            ]

    pl.semaphore_wait(barrier, expected)

    def packet_copy(ds, k):
        return remote(
            packet, packets.at[1 - ds, k], packet_sems, (1 - ds, k), (s + ds, girth_at(k))
        )

    def edge_copy(side):
        return remote(
            edge_out.at[side], edge_in.at[side], edge_sems, (side,), (s, girth_at(2 * side - 1))
        )

    def row_copy(side):
        return remote(
            row_out.at[side],
            row_in.at[side],
            row_sems,
            (side,),
            (s + 2 * side - 1, g),
        )

    for ds in (-1, 1):

        @pl.when(has(ds))
        def _():
            row_copy((ds + 1) // 2).start()
            for k in range(1, n_girth):
                packet_copy(ds, k).start()

    for side in (0, 1):
        edge_copy(side).start()
    for k in range(2, n_girth - 1):
        packet_copy(0, k).start()

    def team_copy(out, into, sems, k):
        q = lax.rem(place + k, TEAM)
        return remote(out.at[q], into.at[place], sems, (k,), (base + q, g))

    def team_arrival(out, into, sems, k):
        return pltpu.make_async_remote_copy(
            src_ref=out.at[place],
            dst_ref=into.at[lax.rem(place + TEAM - k, TEAM)],
            send_sem=sems.at[0, k],
            recv_sem=sems.at[1, k],
            device_id=(base + lax.rem(place + k, TEAM), g),
            device_id_type=MESH,
        )

    far_first = sorted(range(1, TEAM), key=lambda k: -min(k, TEAM - k))

    def own_copy(out, into, n):
        return pltpu.make_async_copy(out.at[place], into.at[place], local_sems.at[n])

    for k in far_first:
        team_copy(inv_out, inv_in, inv_sems, k).start()
    own_copy(inv_out, inv_in, 0).start()

    for side in (0, 1):
        edge_copy(side).wait_recv()
    for k in range(2, n_girth - 1):
        packet_copy(0, k).wait_recv()
    girth_cell = lax.broadcasted_iota(jnp.int32, (8, 128), 0)
    normal_cell = lax.broadcasted_iota(jnp.int32, (8, 128), 1)
    normal_rows = lax.broadcasted_iota(jnp.int32, (128, 128), 0)
    var_row = lax.broadcasted_iota(jnp.int32, (8, 128), 0)
    peer = lax.rem(lane, slots) // CAP

    def packet_from(o, k):
        if o != 1 and k == 0:
            return row_in[1 - o // 2, VARS * 8 :, :]
        if o == 1 and k in (1, n_girth - 1):
            return edge_in[1 if k == 1 else 0, ROWS]
        return packet[...] if k == 0 else packets[o, k]

    def landed(o, plan):
        total = None
        for first in range(0, n_girth, packs):
            tile = packet_from(o, first)
            for k in range(first + 1, first + packs):
                tile = tile + packet_from(o, k)
            code = tile[VARS : VARS + 1, :].astype(jnp.int32) - 1
            row, gc, nc = code >> 10, (code >> 7) & 7, code & 127
            nc = jnp.where(code >= 0, nc, -1)
            tile = jnp.where(var_row == VARS, 1.0, tile)
            part = lax.dot_general(
                jnp.concatenate(plan(tile, row, gc), axis=0),
                jnp.where(normal_rows == nc, 1.0, 0.0),
                (((1,), (1,)), ((), ())),
                precision=PRECISE,
                preferred_element_type=jnp.float32,
            )
            total = part if total is None else total + part
        return total

    def block_rows(r):
        def plan(tile, row, gc):
            here = jnp.logical_and(row == r, peer == g)
            hit = jnp.where(girth_cell == jnp.where(here, gc, -1), 1.0, 0.0)
            return [tile[v : v + 1, :] * hit for v in range(8)]

        return plan

    def own_plan(tile, row, gc):
        rows = block_rows(0)(tile, row, gc) + block_rows(1)(tile, row, gc)
        for at, side in ((7, -1), (0, 1)):
            for r in range(ROWS):
                here = (peer == girth_at(side)) & (row == r) & (gc == at)
                rows.append(tile * jnp.where(here, 1.0, 0.0))
        return rows

    def settle(found, raw):
        hit = found[VARS * 8 : VARS * 8 + 8] > 0.5
        return [jnp.where(hit, found[v * 8 : v * 8 + 8], raw(v)) for v in range(VARS)], hit

    own = landed(1, own_plan)
    cells, fringe = [], []
    for r in range(ROWS):
        found, hit = settle(
            own[r * 64 : r * 64 + 64], lambda v: state[(r * VARS + v) * 8 : (r * VARS + v) * 8 + 8, :]
        )
        cells.append(found)
        fringe.append(hit)
        for v in range(VARS):
            current[(r * VARS + v) * 8 : (r * VARS + v) * 8 + 8, :] = found[v]
    beside = {}
    for side in (0, 1):
        for r in range(ROWS):
            at = 128 + (side * ROWS + r) * 8
            found = own[at : at + 8]
            beside[side, r] = jnp.where(
                found[VARS : VARS + 1] > 0.5, found, edge_in[1 - side, r]
            )
    for ds in (-1, 1):

        @pl.when(has(ds))
        def _():
            row_copy((1 - ds) // 2).wait_recv()
            for k in range(1, n_girth):
                packet_copy(-ds, k).wait_recv()

    outer = []
    for o, r, side in ((0, 1, 1), (2, 0, 0)):
        found, _ = settle(
            landed(o, block_rows(r)), lambda v: row_in[side, v * 8 : v * 8 + 8, :]
        )
        outer.append([jnp.where(has(o - 1), x, 0.0) for x in found])

    for n in (5, 6, 7, 8, 10, 11):
        load(n).wait()
    for r in range(ROWS):
        here = cells[r]
        before = outer[0] if r == 0 else cells[r - 1]
        after = outer[1] if r == ROWS - 1 else cells[r + 1]
        in_disk = disk[r * 8 : r * 8 + 8, :].astype(jnp.float32)
        total = [in_disk * thrust[v] for v in range(VARS)]
        for d in range(6):
            step = []
            for v in range(VARS):
                x = here[v]
                if d == 0:
                    near = before[v]
                elif d == 1:
                    near = after[v]
                elif d == 2:
                    near = jnp.where(girth_cell == 0, beside[0, r][v : v + 1], pltpu.roll(x, 1, 0))
                elif d == 3:
                    near = jnp.where(girth_cell == 7, beside[1, r][v : v + 1], pltpu.roll(x, 7, 0))
                elif d == 4:
                    near = jnp.where(normal_cell == 0, 0.0, pltpu.roll(x, 1, 1))
                else:
                    near = jnp.where(normal_cell == 127, 0.0, pltpu.roll(x, 127, 1))
                step.append(near - x)
            area = face[(r * 6 + d) * 8 : (r * 6 + d) * 8 + 8, :]
            for i in range(VARS):
                flux = step[0] * coupling[d, i, 0]
                for j in range(1, VARS):
                    flux = flux + step[j] * coupling[d, i, j]
                total[i] = total[i] + area * flux
        for v in range(VARS):
            residual_out[(r * VARS + v) * 8 : (r * VARS + v) * 8 + 8, :] = total[v]
            rhs_planes[r, v * 8 : v * 8 + 8, :] = jnp.where(fringe[r], 0.0, -total[v])
        for c in range(8):
            rhs_out[c // PAIR, r, c % PAIR, 0:VARS, :] = rhs_planes[r, pl.ds(c, VARS, stride=8), :]

    for k in far_first:
        team_copy(rhs_out, rhs_in, rhs_sems, k).start()
    own_copy(rhs_out, rhs_in, 1).start()
    keep = [
        pltpu.make_async_copy(new_state, results[0], store_sems.at[0]),
        pltpu.make_async_copy(residual_out, results[1], store_sems.at[1]),
    ]
    keep[1].start()

    def column(k, h, r, j):
        return inv_in[k, h, pl.ds(r * VARS * VARS + j, VARS, stride=VARS), :]

    def matrices(k):
        for r in range(ROWS):
            for h in range(PAIR):
                cols = [column(k, h, r, j) for j in range(VARS)]
                for m in range(VARS):
                    f, b = cols[0] * lower[0, m], cols[0] * upper[0, m]
                    for j in range(1, VARS):
                        f = f + cols[j] * lower[j, m]
                        b = b + cols[j] * upper[j, m]
                    fmap[k, r, h, m, 0:VARS, :] = f
                    bmap[k, r, h, m, 0:VARS, :] = b

    def arrived(step):
        @pl.when(step == 0)
        def _():
            own_copy(inv_out, inv_in, 0).wait()

        for n, k in enumerate(reversed(far_first)):

            @pl.when(step == n + 1)
            def _():
                team_arrival(inv_out, inv_in, inv_sems, k).wait()

    def take_blocks(step, carry):
        arrived(step)
        away = (step + 1) // 2 * (2 * lax.rem(step + 1, 2) - 1)
        matrices(lax.rem(place - away + TEAM, TEAM))
        return carry

    lax.fori_loop(0, TEAM, take_blocks, 0)

    for k in range(1, TEAM):
        team_arrival(rhs_out, rhs_in, rhs_sems, k).wait()
    own_copy(rhs_out, rhs_in, 1).wait()

    def product(matrix, x):
        parts = [matrix(j) * x[j : j + 1, :] for j in range(VARS)]
        return ((parts[0] + parts[1]) + (parts[2] + parts[3])) + (
            (parts[4] + parts[5]) + parts[6]
        )

    offsets = {}
    for k in range(TEAM):
        for r in range(ROWS):
            for h in range(PAIR):
                offsets[k, r, h] = product(
                    lambda j: column(k, h, r, j), rhs_in[k, r, h, 0:VARS, :]
                )

    def link_copy(way):
        return remote(
            link_out.at[way], link_in.at[way], link_sems, (way,), (s + (1 - 2 * way) * TEAM, g)
        )

    def arrive(way, there):
        @pl.when(there)
        def _():
            link_copy(way).wait_recv()

        return [jnp.where(there, link_in[way, h, 0:VARS, :], 0.0) for h in range(PAIR)]

    def depart(way, there, x):
        for h in range(PAIR):
            link_out[way, h, 0:VARS, :] = x[h]

        @pl.when(there)
        def _():
            link_copy(way).start()

    def upd_copy(k):
        q = lax.rem(place + k, TEAM)
        return remote(
            upd_out.at[q],
            upd_in.at[:, pl.ds(pl.multiple_of(place * PAIR * 8, PAIR * 8), PAIR * 8)],
            upd_sems,
            (k,),
            (base + q, g),
        )

    x = arrive(0, team > 0)
    stars = {}
    for k in range(TEAM):
        for r in range(ROWS):
            for h in range(PAIR):
                x[h] = offsets[k, r, h] + product(
                    lambda m: fmap[k, r, h, m, 0:VARS, :], x[h]
                )
                stars[k, r, h] = x[h]
    depart(0, team < n_teams - 1, x)
    x = arrive(1, team < n_teams - 1)
    for k in reversed(range(TEAM)):
        for r in reversed(range(ROWS)):
            for h in range(PAIR):
                x[h] = stars[k, r, h] + product(lambda m: bmap[k, r, h, m, 0:VARS, :], x[h])
                upd_out[k, r, h * 8 : h * 8 + VARS, :] = x[h]
    depart(1, team > 0, x)
    for k in far_first:
        upd_copy(k).start()
    own = pltpu.make_async_copy(
        upd_out.at[place],
        upd_in.at[:, pl.ds(pl.multiple_of(place * PAIR * 8, PAIR * 8), PAIR * 8)],
        local_sems.at[2],
    )
    own.start()
    own.wait()
    for k in range(1, TEAM):
        q = lax.rem(place + TEAM - k, TEAM)
        pltpu.make_async_remote_copy(
            src_ref=upd_out.at[place],
            dst_ref=upd_in.at[:, pl.ds(pl.multiple_of(q * PAIR * 8, PAIR * 8), PAIR * 8)],
            send_sem=upd_sems.at[0, k],
            recv_sem=upd_sems.at[1, k],
            device_id=(base + lax.rem(place + k, TEAM), g),
            device_id_type=MESH,
        ).wait_recv()
    for r in range(ROWS):
        for v in range(VARS):
            at = (r * VARS + v) * 8
            new_state[at : at + 8, :] = current[at : at + 8, :] + upd_in[r, pl.ds(v, 8, stride=8), :]

    keep[0].start()

    for k in range(1, TEAM):
        upd_copy(k).wait_send()
    for side in (0, 1):
        edge_copy(side).wait_send()
    for k in range(2, n_girth - 1):
        packet_copy(0, k).wait_send()
    for ds in (-1, 1):

        @pl.when(has(ds))
        def _():
            row_copy((ds + 1) // 2).wait_send()
            for k in range(1, n_girth):
                packet_copy(ds, k).wait_send()

    for way, there in ((0, team < n_teams - 1), (1, team > 0)):

        @pl.when(there)
        def _():
            link_copy(way).wait_send()

    for copy in keep:
        copy.wait()


def store(a, b, a_out, b_out, a_held, b_held, sems):
    steps = [
        pltpu.make_async_copy(*ends, sems.at[n])
        for n, ends in enumerate(((a, a_held), (b, b_held), (a_held, a_out), (b_held, b_out)))
    ]
    steps[0].start()
    steps[1].start()
    for n in range(2):
        steps[n].wait()
        steps[n + 2].start()
    for n in range(2):
        steps[n + 2].wait()


def per_device(
    state,
    propeller,
    donor_index,
    fringe_index,
    donor_weight,
    disk_mask,
    thrust,
    face,
    coupling,
    diag_inverse,
    lower_jacobian,
    upper_jacobian,
):
    n_stream, n_girth = lax.axis_size("stream"), lax.axis_size("girth")
    f32 = jnp.float32
    hbm = pl.BlockSpec(memory_space=pltpu.HBM)
    blocks = ROWS * VARS * 8
    padded = -(-ROWS * VARS * VARS // 8) * 8
    dma = pltpu.SemaphoreType.DMA
    given = (
        state.reshape(blocks, 128),
        propeller,
        donor_index,
        fringe_index,
        donor_weight,
        disk_mask.reshape(ROWS * 8, 128),
        thrust,
        face.reshape(ROWS * 6 * 8, 128),
        coupling,
        diag_inverse,
        lower_jacobian,
        upper_jacobian,
    )
    scalars = (6, 8, 10, 11)
    held = [
        (pltpu.SMEM if n in scalars else pltpu.VMEM)(x.shape, x.dtype) for n, x in enumerate(given)
    ]
    results = [jax.ShapeDtypeStruct((blocks, 128), f32)] * 2
    new_state, residual = pl.pallas_call(
        functools.partial(kernel, n_stream, n_girth),
        out_shape=results,
        in_specs=[hbm] * 12,
        out_specs=[hbm, hbm],
        scratch_shapes=held
        + [
            pltpu.VMEM((blocks, 128), f32),
            pltpu.VMEM((blocks, 128), f32),
            pltpu.VMEM((8, 128), f32),
            pltpu.VMEM((3, n_girth, 8, 128), f32),
            pltpu.VMEM((2, ROWS + 1, 8, 128), f32),
            pltpu.VMEM((2, ROWS + 1, 8, 128), f32),
            pltpu.VMEM((2, VARS * 8 + 8, 128), f32),
            pltpu.VMEM((2, VARS * 8 + 8, 128), f32),
            pltpu.VMEM((padded * 8, 128), f32),
            pltpu.VMEM((TEAM, PAIR, padded, 128), f32),
            pltpu.VMEM((TEAM, PAIR, padded, 128), f32),
            pltpu.VMEM((blocks, 128), f32),
            pltpu.VMEM((ROWS, VARS * 8, 128), f32),
            pltpu.VMEM((TEAM, ROWS, PAIR, 8, 128), f32),
            pltpu.VMEM((TEAM, ROWS, PAIR, 8, 128), f32),
            pltpu.VMEM((TEAM, ROWS, PAIR, VARS, 8, 128), f32),
            pltpu.VMEM((TEAM, ROWS, PAIR, VARS, 8, 128), f32),
            pltpu.VMEM((TEAM, ROWS, PAIR * 8, 128), f32),
            pltpu.VMEM((ROWS, TEAM * PAIR * 8, 128), f32),
            pltpu.VMEM((2, PAIR, 8, 128), f32),
            pltpu.VMEM((2, PAIR, 8, 128), f32),
            dma((2, 3, n_girth)),
            dma((2, 2)),
            dma((2, 2)),
            dma((2, TEAM)),
            dma((2, TEAM)),
            dma((2, TEAM)),
            dma((2, 2)),
            dma((3,)),
            dma((12,)),
            dma((2,)),
        ],
        compiler_params=pltpu.CompilerParams(
            collective_id=0, has_side_effects=True, vmem_limit_bytes=60 * 1024 * 1024
        ),
        cost_estimate=pl.CostEstimate(flops=12_000_000, bytes_accessed=500_000, transcendentals=0),
    )(*given)
    new_state, residual = pl.pallas_call(
        store,
        out_shape=results,
        in_specs=[hbm, hbm],
        out_specs=[hbm, hbm],
        scratch_shapes=[pltpu.VMEM((blocks, 128), f32)] * 2 + [dma((4,))],
        compiler_params=pltpu.CompilerParams(vmem_limit_bytes=60 * 1024 * 1024),
    )(new_state, residual)
    return new_state.reshape(state.shape), residual.reshape(state.shape)


def solution(mesh):
    placed = (
        P("stream", None, "girth", None),
        P(None, ("stream", "girth")),
        P(("stream", "girth"), None),
        P(("stream", "girth"), None),
        P(("stream", "girth"), None),
        P("stream", "girth", None),
        P(),
        P("stream", None, "girth", None),
        P(),
        P("stream", None, None, "girth", None),
        P(),
        P(),
    )
    return jax.shard_map(
        per_device,
        mesh=mesh,
        in_specs=placed,
        out_specs=(P("stream", None, "girth", None), P("stream", None, "girth", None)),
        check_vma=False,
    )
```
